32 devices in a mesh: groups: 2 (over y), rows: 4 (over z), pairs: 2 (over x), sub: 2 (over core).
Axes of the slice: x: 2, y: 2, z: 4, core: 2. Of those that a mesh axis runs over, the one named last changes fastest.
Arguments:
- embeddings: bfloat16 [16384, 768], P(('groups', 'rows')), parts along dimension 0
- slot: int32 [16384], P(('groups', 'rows')), parts along dimension 0, may hold values from 0 to 8191, as said below
- list_id: int32 [16384], P(('groups', 'rows')), parts along dimension 0, may hold values from 0 to 7, as said below
Outputs:
- max_similarity: float32 [16384], P(('groups', 'rows')), parts along dimension 0
The draws below stay inside these ranges and needn't reach their ends.
There are 2 independent parts, one for each index of `groups`. The reference program is written for one: setup_inputs(seed, part) draws one part's arguments, and reference() takes and returns one part's arrays. A program takes and returns all parts, laid end to end along the dimension named above; each array names one. Nothing has to cross between parts.
Inputs may be any that keep to these rules, and one draw needn't show every extreme that they name: `slot`: A permutation. Positions 2048 * b to 2048 * (b + 1) - 1 form owner block b; of the images of one home shard, 256, 512 or 768 lie in each owner block, the largest count in every draw. `list_id`: never falls along the positions; every id holds a contiguous run of 1 to 6144 positions, and one run has exactly that length.
All inputs are finite; a program needn't handle non-finite values.
Results may differ from the reference program's by a relative error of at most 0.00054.
Values may be sent and summed in bfloat16 or wider, within the bound.
No kernel may reach another device: no remote copies, remote signals or barrier semaphores. Data moves between devices by JAX's collectives and lax.ppermute only.
A program may use at most 64 MiB of HBM per device.

```python
import jax
import jax.numpy as jnp
from jax import lax

D = 768
ROWS_DEV = 2048
SPAN = 4
IMAGES = 8192
CLUSTERS = 8


def layout(key):
    peers = IMAGES // ROWS_DEV
    base = ROWS_DEV // peers
    half = base // 2
    keys = jax.random.split(key, 7)
    first = jax.random.permutation(keys[0], peers)
    second = jnp.roll(first, -1)
    index = jnp.arange(peers)
    counts = base + half * ((index[None, :] == first[:, None]).astype(jnp.int32) - (index[None, :] == second[:, None]).astype(jnp.int32))
    ends = jnp.cumsum(counts, axis=1)
    starts = ends - counts
    ranks = jnp.arange(ROWS_DEV)
    target = jnp.sum((ends[:, None, :] <= ranks[None, :, None]).astype(jnp.int32), axis=2)
    within = ranks[None, :] - jnp.take_along_axis(starts, target, axis=1)
    before = jnp.cumsum(counts, axis=0) - counts
    offset = jnp.take_along_axis(before, target, axis=1) + within
    owner_perm = jax.vmap(lambda sub_key: jax.random.permutation(sub_key, ROWS_DEV))(jax.random.split(keys[1], peers))
    by_rank = target * ROWS_DEV + owner_perm[target, offset]
    home_perm = jax.vmap(lambda sub_key: jax.random.permutation(sub_key, ROWS_DEV))(jax.random.split(keys[2], peers))
    inverse = jnp.argsort(home_perm, axis=1)
    slots = jnp.take_along_axis(by_rank, inverse, axis=1).reshape(IMAGES).astype(jnp.int32)
    reach = (SPAN - 1) * ROWS_DEV
    anchor = jax.random.randint(keys[3], (), 1, ROWS_DEV)
    position = jnp.arange(IMAGES)
    mandatory = (position >= anchor) & ((position - anchor) % reach == 0)
    count_fixed = jnp.sum(mandatory.astype(jnp.int32))
    full = (IMAGES - anchor) // reach
    zone = jax.random.randint(keys[4], (), 0, full)
    zone_low = anchor + zone * reach
    inside = (position > zone_low) & (position < zone_low + reach)
    eligible = (position >= 1) & jnp.logical_not(mandatory) & jnp.logical_not(inside)
    pair_free = eligible[0::2] & eligible[1::2]
    pair_scores = jnp.where(pair_free, jax.random.permutation(keys[6], IMAGES // 2), -1)
    singles = lax.top_k(pair_scores, 2)[1]
    single_cut = jnp.zeros((IMAGES,), jnp.int32).at[2 * singles].set(1).at[2 * singles + 1].set(1)
    remaining = eligible & (single_cut == 0)
    scores = jnp.where(remaining, jax.random.permutation(keys[5], IMAGES), -1)
    extra_most = CLUSTERS - 5 - (IMAGES - 1) // reach
    chosen = lax.top_k(scores, extra_most)[1]
    keep = (jnp.arange(extra_most) < CLUSTERS - 5 - count_fixed).astype(jnp.int32)
    cuts = jnp.maximum(mandatory.astype(jnp.int32), single_cut).at[chosen].max(keep)
    clusters = (jnp.cumsum(cuts) - cuts[0]).astype(jnp.int32)
    return (slots, clusters, zone_low, anchor)


def draw_slot(key, part):
    slots, clusters, zone_low, anchor = layout(key)
    return slots


def draw_list_id(key, part):
    slots, clusters, zone_low, anchor = layout(key)
    return clusters


def draw_embeddings(key, part):
    slots, clusters, zone_low, anchor = layout(key)
    key = jax.random.fold_in(key, 11)
    keys = jax.random.split(key, 6)
    basis = jax.random.normal(keys[0], (IMAGES, D), jnp.float32)
    scales = jnp.exp(jax.random.uniform(keys[4], (IMAGES,), jnp.float32, jnp.log(0.5), jnp.log(4.0)))
    reach = (SPAN - 1) * ROWS_DEV
    distance = jax.random.randint(keys[1], (IMAGES,), 1, reach)
    position = jnp.arange(IMAGES)
    tail_start = (zone_low // ROWS_DEV + SPAN - 1) * ROWS_DEV
    gap = ROWS_DEV - anchor
    tail = (position >= tail_start) & (position < zone_low + reach)
    head = (position >= zone_low) & (position < zone_low + jnp.minimum(anchor, gap))
    forced_partner = zone_low + (position - tail_start) % gap
    partner = jnp.where(tail, forced_partner, jnp.maximum(position - distance, 0))
    coin = jax.random.randint(keys[2], (IMAGES,), 0, 2) == 1
    paired = tail | (clusters[partner] == clusters) & (position - distance >= 0) & coin & jnp.logical_not(head)
    strength = jnp.where(tail, jax.random.uniform(keys[5], (IMAGES,), jnp.float32, 0.6, 0.97), jax.random.uniform(keys[3], (IMAGES,), jnp.float32, 0.3, 0.97))
    mixing = strength * paired.astype(jnp.float32)
    mixed = mixing[:, None] * basis[partner] + jnp.sqrt(1.0 - mixing * mixing)[:, None] * basis
    return (mixed * scales[:, None])[slots].astype(jnp.bfloat16)


def setup_inputs(seed: int = 0, part: int = 0) -> dict:
    streams_of = jax.random.split(jax.random.key(seed), 4)
    part_keys = jax.random.split(jax.random.fold_in(streams_of[3], part), 4)
    embeddings = draw_embeddings(jax.random.fold_in(jax.random.fold_in(streams_of[3], part), 71), part)
    slot = draw_slot(jax.random.fold_in(jax.random.fold_in(streams_of[3], part), 71), part)
    list_id = draw_list_id(jax.random.fold_in(jax.random.fold_in(streams_of[3], part), 71), part)
    return dict(embeddings=embeddings, slot=slot, list_id=list_id)


def reference(embeddings, slot, list_id):
    wide = embeddings.astype(jnp.float32)
    unit = (wide / jnp.sqrt(lax.optimization_barrier(jnp.sum(wide * wide, axis=1, keepdims=True)) + 1e-06)).astype(jnp.bfloat16)
    ordered = jnp.zeros_like(unit).at[slot].set(unit)
    tags = (list_id + 1).astype(jnp.int32)
    reach = (SPAN - 1) * ROWS_DEV
    padded = jnp.pad(ordered, ((0, reach), (0, 0)))
    padded_tags = jnp.pad(tags, (0, reach))
    blocks = IMAGES // ROWS_DEV
    window = ROWS_DEV + reach

    def one_block(best, index):
        start = (index * ROWS_DEV).astype(jnp.int32)
        rows_here = lax.dynamic_slice_in_dim(padded, start, ROWS_DEV, 0)
        tags_here = lax.dynamic_slice_in_dim(padded_tags, start, ROWS_DEV, 0)
        others = lax.dynamic_slice_in_dim(padded, start, window, 0)
        other_tags = lax.dynamic_slice_in_dim(padded_tags, start, window, 0)
        scores = jnp.dot(rows_here, others.T, preferred_element_type=jnp.float32)
        row_pos = jnp.arange(ROWS_DEV, dtype=jnp.int32)
        col_pos = jnp.arange(window, dtype=jnp.int32)
        mask = (tags_here[:, None] == other_tags[None, :]) & (row_pos[:, None] != col_pos[None, :])
        masked = jnp.where(mask, scores, jnp.float32(-1.0))
        column_part = lax.dynamic_slice_in_dim(best, start, window, 0)
        column_part = jnp.maximum(column_part, lax.optimization_barrier(jnp.max(masked, axis=0)))
        best = lax.dynamic_update_slice_in_dim(best, column_part, start, 0)
        row_part = lax.dynamic_slice_in_dim(best, start, ROWS_DEV, 0)
        best = lax.dynamic_update_slice_in_dim(best, jnp.maximum(row_part, lax.optimization_barrier(jnp.max(masked, axis=1))), start, 0)
        return (best, None)
    initial = jnp.full((IMAGES + reach,), -1.0, jnp.float32)
    best, _ = lax.scan(one_block, initial, jnp.arange(blocks, dtype=jnp.int32))
    return best[:IMAGES][slot]
```

```python
import functools

import jax
import jax.numpy as jnp
from jax import lax
from jax.experimental import pallas as pl
from jax.experimental.pallas import tpu as pltpu
from jax.sharding import PartitionSpec as P

SPAN = 4
POSITIONS_PER_CLUSTER = 1024
LANES = 128
TILE = 256
WIDE_MOVES = ((0, 3), (1, 2), (2, 0), (3, 1))
NEAR_MOVES = ((0, 1), (3, 2))


def shifted(value, axis, by):
    length = lax.axis_size(axis)
    pairs = [(i, i + by) for i in range(length) if 0 <= i + by < length]
    return lax.ppermute(value, axis, pairs)


def placed(received, codes, rows_dev):
    flat = received.reshape(-1, received.shape[-1])
    flat_codes = codes.reshape(-1)
    target = jnp.where(flat_codes >= 0, flat_codes, rows_dev)
    return jnp.zeros((rows_dev, flat.shape[1]), flat.dtype).at[target].set(flat, mode="drop")


def masked_scores(owned, tags, far_rows, far_tags):
    scores = lax.dot_general(
        owned, far_rows, (((1,), (1,)), ((), ())), preferred_element_type=jnp.float32
    )
    return jnp.where(tags[:, None] == far_tags[None, :], scores, -1.0)


def banded(embeddings, slot, list_id):
    rows_dev = embeddings.shape[0]
    width = embeddings.shape[1]
    peers = lax.axis_size("rows")
    capacity = 3 * (rows_dev // peers) // 2
    wide = embeddings.astype(jnp.float32)
    unit = (wide / jnp.sqrt(jnp.sum(wide * wide, axis=1, keepdims=True) + 1e-06)).astype(
        jnp.bfloat16
    )
    owner = slot // rows_dev
    local = slot - owner * rows_dev
    onehot = (owner[:, None] == jnp.arange(peers, dtype=jnp.int32)[None, :]).astype(jnp.int32)
    order = jnp.sum((jnp.cumsum(onehot, axis=0) - onehot) * onehot, axis=1)
    send_code = jnp.full((peers, capacity), -1, jnp.int32).at[owner, order].set(local)
    pieces = lax.axis_size(("pairs", "sub"))
    which = lax.axis_index(("pairs", "sub"))
    send_rows = jnp.zeros((peers, capacity, width), jnp.bfloat16).at[owner, order].set(unit)
    got_rows, got_code = (
        lax.all_to_all(send_rows, "rows", split_axis=0, concat_axis=0, tiled=True),
        lax.all_to_all(send_code, "rows", split_axis=0, concat_axis=0, tiled=True),
    )
    owned = placed(got_rows, got_code, rows_dev)
    tags = list_id + 1
    band = rows_dev // pieces
    columns = lax.dynamic_slice_in_dim(owned, which * band, band, 0)
    column_tags = lax.dynamic_slice_in_dim(tags, which * band, band, 0)
    row_index = jnp.arange(rows_dev, dtype=jnp.int32)
    column_index = which * band + jnp.arange(band, dtype=jnp.int32)
    near = masked_scores(owned, tags, columns, column_tags)
    near = jnp.where(row_index[:, None] == column_index[None, :], -1.0, near)
    best = jnp.max(near, axis=1)
    offsets = list(range(1 - SPAN, 0)) + list(range(1, SPAN))
    for step in offsets:
        far_rows, far_tags = shifted((columns, column_tags), "rows", step)
        best = jnp.maximum(best, jnp.max(masked_scores(owned, tags, far_rows, far_tags), axis=1))
    answer = lax.pmax(best, ("pairs", "sub"))
    values = jnp.where(got_code >= 0, answer[jnp.clip(got_code, 0, rows_dev - 1)], 0.0)
    homeward = lax.all_to_all(values, "rows", split_axis=0, concat_axis=0, tiled=True)
    return homeward[owner, order]


def normalised(rows):
    wide = rows.astype(jnp.float32)
    squares = jnp.sum(wide * wide, axis=1, keepdims=True)
    return (wide * (1.0 / jnp.sqrt(squares + 1e-06))).astype(jnp.bfloat16)


def unit_kernel(rows_ref, unit_ref):
    unit_ref[...] = normalised(rows_ref[...])


def unit_rows(rows):
    count, width = rows.shape
    step = min(count, 512)
    return pl.pallas_call(
        unit_kernel,
        grid=(count // step,),
        in_specs=[pl.BlockSpec((step, width), lambda i: (i, 0))],
        out_specs=pl.BlockSpec((step, width), lambda i: (i, 0)),
        out_shape=jax.ShapeDtypeStruct(rows.shape, jnp.bfloat16),
        cost_estimate=pl.CostEstimate(
            flops=4 * count * width, bytes_accessed=4 * count * width, transcendentals=count
        ),
    )(rows)


def meet_kernel(same, which_ref, other_ref, other_tags_ref, home_ref, home_tags_ref, home_best_ref, other_best_ref):
    others, homes = other_ref.shape[0], home_ref.shape[0]
    unit = normalised(other_ref[...])
    tags = other_tags_ref[...][:, :1]
    folded = jnp.full((others, LANES), -1.0, jnp.float32)
    if same:
        place = which_ref[0] * others + lax.broadcasted_iota(jnp.int32, (others, TILE), 0)
    for start in range(0, homes, TILE):
        scores = lax.dot_general(
            unit,
            home_ref[pl.ds(start, TILE), :],
            (((1,), (1,)), ((), ())),
            preferred_element_type=jnp.float32,
        )
        keep = tags == home_tags_ref[:, pl.ds(start, TILE)]
        if same:
            keep &= place != start + lax.broadcasted_iota(jnp.int32, (others, TILE), 1)
        scores = jnp.where(keep, scores, -1.0)
        home_best_ref[:, pl.ds(start, TILE)] = jnp.max(scores, axis=0, keepdims=True)
        for lane in range(0, TILE, LANES):
            folded = jnp.maximum(folded, scores[:, lane : lane + LANES])
    other_best_ref[...] = jnp.max(folded.T, axis=0, keepdims=True)


def meet(others, other_tags, homes, home_tags, which, same=False):
    count, width = others.shape
    total = homes.shape[0]
    vmem = pl.BlockSpec(memory_space=pltpu.VMEM)
    home_best, other_best = pl.pallas_call(
        functools.partial(meet_kernel, same),
        in_specs=[pl.BlockSpec(memory_space=pltpu.SMEM), vmem, vmem, vmem, vmem],
        out_specs=[vmem, vmem],
        out_shape=[
            jax.ShapeDtypeStruct((1, total), jnp.float32),
            jax.ShapeDtypeStruct((1, count), jnp.float32),
        ],
        compiler_params=pltpu.CompilerParams(vmem_limit_bytes=32 * 1024 * 1024),
        cost_estimate=pl.CostEstimate(
            flops=2 * count * total * width,
            bytes_accessed=2 * (count + total) * width,
            transcendentals=count,
        ),
    )(
        which.reshape(1),
        others,
        jnp.broadcast_to(other_tags[:, None], (count, LANES)),
        homes,
        home_tags.reshape(1, total),
    )
    return home_best.reshape(total), other_best.reshape(count)


def dense(embeddings, slot, list_id):
    rows_dev = embeddings.shape[0]
    peers = lax.axis_size("rows")
    me = lax.axis_index("rows")
    pieces = lax.axis_size(("pairs", "sub"))
    which = lax.axis_index(("pairs", "sub"))
    band = rows_dev // pieces
    clusters = peers * rows_dev // POSITIONS_PER_CLUSTER

    def origin(moves):
        source = [peers] * peers
        for sender, receiver in moves:
            source[receiver] = sender
        return jnp.array(source, jnp.int32)[me]

    def back(value, moves):
        returned = lax.ppermute(value, "rows", [(b, a) for a, b in moves])
        senders = [a for a, _ in moves]
        if len(senders) < peers:
            sent = functools.reduce(jnp.logical_or, [me == a for a in senders])
            returned = jnp.where(sent, returned, -1.0)
        return returned

    quarter = lax.dynamic_slice_in_dim(embeddings, which * band, band, 0)
    wide_rows = lax.ppermute(quarter, "rows", WIDE_MOVES)
    near_rows = lax.ppermute(quarter, "rows", NEAR_MOVES)

    gathered = lax.all_gather(jnp.stack([slot, list_id]), "rows")
    slots, lists = gathered[:, 0], gathered[:, 1]
    starts = [jnp.sum((lists < k).astype(jnp.int32)) for k in range(1, clusters)]

    def tags_of(positions):
        return sum((positions >= start).astype(jnp.int32) for start in starts)

    home_tags = tags_of(slot)

    def quarter_tags(source):
        block = lax.dynamic_slice(slots, (jnp.minimum(source, peers - 1), which * band), (1, band))
        return jnp.where(source < peers, tags_of(block.reshape(band)), -1)

    homes = unit_rows(embeddings)
    own_tags = lax.dynamic_slice_in_dim(home_tags, which * band, band, 0)
    best, _ = meet(quarter, own_tags, homes, home_tags, which, same=True)
    near_best, near_back = meet(near_rows, quarter_tags(origin(NEAR_MOVES)), homes, home_tags, which)
    wide_best, wide_back = meet(wide_rows, quarter_tags(origin(WIDE_MOVES)), homes, home_tags, which)
    returned = jnp.maximum(back(near_back, NEAR_MOVES), back(wide_back, WIDE_MOVES))
    best = jnp.maximum(best, jnp.maximum(near_best, wide_best))
    mine = lax.dynamic_slice_in_dim(best, which * band, band, 0)
    best = lax.dynamic_update_slice_in_dim(best, jnp.maximum(mine, returned), which * band, 0)
    return lax.pmax(best, ("pairs", "sub"))


def on_device(embeddings, slot, list_id):
    if lax.axis_size("rows") == SPAN:
        return dense(embeddings, slot, list_id)
    return banded(embeddings, slot, list_id)


def solution(mesh):
    return jax.shard_map(
        on_device,
        mesh=mesh,
        in_specs=(P(("groups", "rows"), None), P(("groups", "rows")), P(("groups", "rows"))),
        out_specs=P(("groups", "rows")),
        check_vma=False,
    )
```

```python
import functools

import jax
import jax.numpy as jnp
from jax import lax
from jax.experimental import pallas as pl
from jax.experimental.pallas import tpu as pltpu
from jax.sharding import PartitionSpec as P

SPAN = 4
POSITIONS_PER_CLUSTER = 1024
LANES = 128
TILE = 256


def shifted(value, axis, by):
    length = lax.axis_size(axis)
    pairs = [(i, i + by) for i in range(length) if 0 <= i + by < length]
    return lax.ppermute(value, axis, pairs)


def placed(received, codes, rows_dev):
    flat = received.reshape(-1, received.shape[-1])
    flat_codes = codes.reshape(-1)
    target = jnp.where(flat_codes >= 0, flat_codes, rows_dev)
    return jnp.zeros((rows_dev, flat.shape[1]), flat.dtype).at[target].set(flat, mode="drop")


def masked_scores(owned, tags, far_rows, far_tags):
    scores = lax.dot_general(
        owned, far_rows, (((1,), (1,)), ((), ())), preferred_element_type=jnp.float32
    )
    return jnp.where(tags[:, None] == far_tags[None, :], scores, -1.0)


def banded(embeddings, slot, list_id):
    rows_dev = embeddings.shape[0]
    width = embeddings.shape[1]
    peers = lax.axis_size("rows")
    capacity = 3 * (rows_dev // peers) // 2
    wide = embeddings.astype(jnp.float32)
    unit = (wide / jnp.sqrt(jnp.sum(wide * wide, axis=1, keepdims=True) + 1e-06)).astype(
        jnp.bfloat16
    )
    owner = slot // rows_dev
    local = slot - owner * rows_dev
    onehot = (owner[:, None] == jnp.arange(peers, dtype=jnp.int32)[None, :]).astype(jnp.int32)
    order = jnp.sum((jnp.cumsum(onehot, axis=0) - onehot) * onehot, axis=1)
    send_code = jnp.full((peers, capacity), -1, jnp.int32).at[owner, order].set(local)
    pieces = lax.axis_size(("pairs", "sub"))
    which = lax.axis_index(("pairs", "sub"))
    send_rows = jnp.zeros((peers, capacity, width), jnp.bfloat16).at[owner, order].set(unit)
    got_rows, got_code = (
        lax.all_to_all(send_rows, "rows", split_axis=0, concat_axis=0, tiled=True),
        lax.all_to_all(send_code, "rows", split_axis=0, concat_axis=0, tiled=True),
    )
    owned = placed(got_rows, got_code, rows_dev)
    tags = list_id + 1
    band = rows_dev // pieces
    columns = lax.dynamic_slice_in_dim(owned, which * band, band, 0)
    column_tags = lax.dynamic_slice_in_dim(tags, which * band, band, 0)
    row_index = jnp.arange(rows_dev, dtype=jnp.int32)
    column_index = which * band + jnp.arange(band, dtype=jnp.int32)
    near = masked_scores(owned, tags, columns, column_tags)
    near = jnp.where(row_index[:, None] == column_index[None, :], -1.0, near)
    best = jnp.max(near, axis=1)
    offsets = list(range(1 - SPAN, 0)) + list(range(1, SPAN))
    for step in offsets:
        far_rows, far_tags = shifted((columns, column_tags), "rows", step)
        best = jnp.maximum(best, jnp.max(masked_scores(owned, tags, far_rows, far_tags), axis=1))
    answer = lax.pmax(best, ("pairs", "sub"))
    values = jnp.where(got_code >= 0, answer[jnp.clip(got_code, 0, rows_dev - 1)], 0.0)
    homeward = lax.all_to_all(values, "rows", split_axis=0, concat_axis=0, tiled=True)
    return homeward[owner, order]


def normalised(rows):
    wide = rows.astype(jnp.float32)
    squares = jnp.sum(wide * wide, axis=1, keepdims=True)
    return (wide * (1.0 / jnp.sqrt(squares + 1e-06))).astype(jnp.bfloat16)


def unit_kernel(rows_ref, unit_ref):
    unit_ref[...] = normalised(rows_ref[...])


def unit_rows(rows):
    count, width = rows.shape
    step = min(count, 512)
    return pl.pallas_call(
        unit_kernel,
        grid=(count // step,),
        in_specs=[pl.BlockSpec((step, width), lambda i: (i, 0))],
        out_specs=pl.BlockSpec((step, width), lambda i: (i, 0)),
        out_shape=jax.ShapeDtypeStruct(rows.shape, jnp.bfloat16),
        cost_estimate=pl.CostEstimate(
            flops=4 * count * width, bytes_accessed=4 * count * width, transcendentals=count
        ),
    )(rows)


def tags_kernel(clusters, place_ref, own_ref, slot_ref, *refs):
    passed_refs, (home_ref, own_tags_ref, left_tags_ref, across_tags_ref) = refs[:-4], refs[-4:]
    which, receives = place_ref[0], place_ref[1]
    half = own_ref.shape[0] // 2
    starts = []
    for k in range(1, clusters):
        starts.append(jnp.sum(sum((ref[:half, :] < k).astype(jnp.int32) for ref in passed_refs)))

    def tags_of(positions):
        return sum((positions >= start).astype(jnp.int32) for start in starts)

    def column(tags):
        return jnp.broadcast_to(tags, (LANES, tags.shape[1])).T

    def arrived(piece):
        slots = passed_refs[0][pl.ds(half + which, 1), :]
        for flip in range(1, len(passed_refs)):
            slots = jnp.where(which == piece ^ flip, passed_refs[flip][pl.ds(half + which, 1), :], slots)
        return tags_of(slots)

    home_ref[...] = tags_of(slot_ref[...])
    own_tags_ref[...] = column(tags_of(own_ref[pl.ds(half + which, 1), :]))
    left_tags_ref[...] = column(arrived(0))
    across_tags_ref[...] = column(jnp.where(receives == 1, arrived(1), -1))


def tags_for(clusters, which, receives, own, slot, passed):
    band, total = own.shape[1], slot.shape[0]
    vmem = pl.BlockSpec(memory_space=pltpu.VMEM)
    columns = jax.ShapeDtypeStruct((band, LANES), jnp.int32)
    return pl.pallas_call(
        functools.partial(tags_kernel, clusters),
        in_specs=[pl.BlockSpec(memory_space=pltpu.SMEM)] + [vmem] * (2 + len(passed)),
        out_specs=[vmem] * 4,
        out_shape=[jax.ShapeDtypeStruct((1, total), jnp.int32)] + [columns] * 3,
        cost_estimate=pl.CostEstimate(flops=total * 32, bytes_accessed=total * 32, transcendentals=0),
    )(jnp.stack([which, receives.astype(jnp.int32)]), own, slot.reshape(1, total), *passed)


def meet_kernel(same, ready, which_ref, other_ref, other_tags_ref, home_ref, home_tags_ref, home_best_ref, other_best_ref):
    others, homes = other_ref.shape[0], home_ref.shape[0]
    unit = other_ref[...] if ready else normalised(other_ref[...])
    tags = other_tags_ref[...][:, :1]
    folded = jnp.full((others, LANES), -1.0, jnp.float32)
    if same:
        place = which_ref[0] * others + lax.broadcasted_iota(jnp.int32, (others, TILE), 0)
    for start in range(0, homes, TILE):
        scores = lax.dot_general(
            unit,
            home_ref[pl.ds(start, TILE), :],
            (((1,), (1,)), ((), ())),
            preferred_element_type=jnp.float32,
        )
        keep = tags == home_tags_ref[:, pl.ds(start, TILE)]
        if same:
            keep &= place != start + lax.broadcasted_iota(jnp.int32, (others, TILE), 1)
        scores = jnp.where(keep, scores, -1.0)
        home_best_ref[:, pl.ds(start, TILE)] = jnp.max(scores, axis=0, keepdims=True)
        for lane in range(0, TILE, LANES):
            folded = jnp.maximum(folded, scores[:, lane : lane + LANES])
    other_best_ref[...] = jnp.max(folded.T, axis=0, keepdims=True)


def meet(others, other_tags, homes, home_tags, which, same=False, ready=False):
    count, width = others.shape
    total = homes.shape[0]
    vmem = pl.BlockSpec(memory_space=pltpu.VMEM)
    home_best, other_best = pl.pallas_call(
        functools.partial(meet_kernel, same, ready),
        in_specs=[pl.BlockSpec(memory_space=pltpu.SMEM), vmem, vmem, vmem, vmem],
        out_specs=[vmem, vmem],
        out_shape=[
            jax.ShapeDtypeStruct((1, total), jnp.float32),
            jax.ShapeDtypeStruct((1, count), jnp.float32),
        ],
        compiler_params=pltpu.CompilerParams(vmem_limit_bytes=32 * 1024 * 1024),
        cost_estimate=pl.CostEstimate(
            flops=2 * count * total * width,
            bytes_accessed=2 * (count + total) * width,
            transcendentals=count,
        ),
    )(which.reshape(1), others, other_tags, homes, home_tags)
    return home_best.reshape(total), other_best.reshape(count)


def dense(embeddings, slot, list_id):
    rows_dev = embeddings.shape[0]
    peers = lax.axis_size("rows")
    me = lax.axis_index("rows")
    pieces = lax.axis_size(("pairs", "sub"))
    which = lax.axis_index(("pairs", "sub"))
    band = rows_dev // pieces
    clusters = peers * rows_dev // POSITIONS_PER_CLUSTER
    round_moves = [(i, (i + 1) % peers) for i in range(peers)]
    across_moves = [(0, 2), (3, 1)]

    def moved(value, moves):
        return lax.ppermute(value, "rows", moves)

    def returned(value, moves):
        return lax.ppermute(value, "rows", [(b, a) for a, b in moves])

    message = jnp.concatenate([list_id.reshape(pieces, band), slot.reshape(pieces, band)])
    passed = lax.ppermute(
        message,
        ("rows", "pairs", "sub"),
        [
            (i * pieces + p, (i + p + 1) % peers * pieces + p)
            for i in range(peers)
            for p in range(pieces)
        ],
    )
    quarter, embeddings, passed = lax.optimization_barrier(
        (lax.dynamic_slice_in_dim(embeddings, which * band, band, 0), embeddings, passed)
    )
    round_rows = moved(quarter, round_moves)
    passed = [passed] + [
        lax.ppermute(passed, ("pairs", "sub"), [(p, p ^ flip) for p in range(pieces)])
        for flip in range(1, pieces)
    ]

    homes = unit_rows(embeddings)
    across_rows = moved(lax.dynamic_slice_in_dim(homes, which * band, band, 0), across_moves)
    receives = (me == 1) | (me == 2)
    home_tags, own_tags, round_tags, across_tags = tags_for(
        clusters, which, receives, message, slot, passed
    )
    best, _ = meet(quarter, own_tags, homes, home_tags, which, same=True)
    round_best, round_back = meet(round_rows, round_tags, homes, home_tags, which)
    across_best, across_back = meet(across_rows, across_tags, homes, home_tags, which, ready=True)
    back = jnp.maximum(
        returned(round_back, round_moves),
        jnp.where(receives, -1.0, returned(across_back, across_moves)),
    )
    best = jnp.maximum(best, jnp.maximum(round_best, across_best))
    mine = lax.dynamic_slice_in_dim(best, which * band, band, 0)
    best = lax.dynamic_update_slice_in_dim(best, jnp.maximum(mine, back), which * band, 0)
    return lax.pmax(best, ("pairs", "sub"))


def on_device(embeddings, slot, list_id):
    if lax.axis_size("rows") == SPAN:
        return dense(embeddings, slot, list_id)
    return banded(embeddings, slot, list_id)


def solution(mesh):
    return jax.shard_map(
        on_device,
        mesh=mesh,
        in_specs=(P(("groups", "rows"), None), P(("groups", "rows")), P(("groups", "rows"))),
        out_specs=P(("groups", "rows")),
        check_vma=False,
    )
```

```python
import functools

import jax
import jax.numpy as jnp
from jax import lax
from jax.experimental import pallas as pl
from jax.experimental.pallas import tpu as pltpu
from jax.sharding import PartitionSpec as P

SPAN = 4
POSITIONS_PER_CLUSTER = 1024
LANES = 128
TILE = 256


def shifted(value, axis, by):
    length = lax.axis_size(axis)
    pairs = [(i, i + by) for i in range(length) if 0 <= i + by < length]
    return lax.ppermute(value, axis, pairs)


def placed(received, codes, rows_dev):
    flat = received.reshape(-1, received.shape[-1])
    flat_codes = codes.reshape(-1)
    target = jnp.where(flat_codes >= 0, flat_codes, rows_dev)
    return jnp.zeros((rows_dev, flat.shape[1]), flat.dtype).at[target].set(flat, mode="drop")


def masked_scores(owned, tags, far_rows, far_tags):
    scores = lax.dot_general(
        owned, far_rows, (((1,), (1,)), ((), ())), preferred_element_type=jnp.float32
    )
    return jnp.where(tags[:, None] == far_tags[None, :], scores, -1.0)


def banded(embeddings, slot, list_id):
    rows_dev = embeddings.shape[0]
    width = embeddings.shape[1]
    peers = lax.axis_size("rows")
    capacity = 3 * (rows_dev // peers) // 2
    wide = embeddings.astype(jnp.float32)
    unit = (wide / jnp.sqrt(jnp.sum(wide * wide, axis=1, keepdims=True) + 1e-06)).astype(
        jnp.bfloat16
    )
    owner = slot // rows_dev
    local = slot - owner * rows_dev
    onehot = (owner[:, None] == jnp.arange(peers, dtype=jnp.int32)[None, :]).astype(jnp.int32)
    order = jnp.sum((jnp.cumsum(onehot, axis=0) - onehot) * onehot, axis=1)
    send_code = jnp.full((peers, capacity), -1, jnp.int32).at[owner, order].set(local)
    pieces = lax.axis_size(("pairs", "sub"))
    which = lax.axis_index(("pairs", "sub"))
    send_rows = jnp.zeros((peers, capacity, width), jnp.bfloat16).at[owner, order].set(unit)
    got_rows, got_code = (
        lax.all_to_all(send_rows, "rows", split_axis=0, concat_axis=0, tiled=True),
        lax.all_to_all(send_code, "rows", split_axis=0, concat_axis=0, tiled=True),
    )
    owned = placed(got_rows, got_code, rows_dev)
    tags = list_id + 1
    band = rows_dev // pieces
    columns = lax.dynamic_slice_in_dim(owned, which * band, band, 0)
    column_tags = lax.dynamic_slice_in_dim(tags, which * band, band, 0)
    row_index = jnp.arange(rows_dev, dtype=jnp.int32)
    column_index = which * band + jnp.arange(band, dtype=jnp.int32)
    near = masked_scores(owned, tags, columns, column_tags)
    near = jnp.where(row_index[:, None] == column_index[None, :], -1.0, near)
    best = jnp.max(near, axis=1)
    offsets = list(range(1 - SPAN, 0)) + list(range(1, SPAN))
    for step in offsets:
        far_rows, far_tags = shifted((columns, column_tags), "rows", step)
        best = jnp.maximum(best, jnp.max(masked_scores(owned, tags, far_rows, far_tags), axis=1))
    answer = lax.pmax(best, ("pairs", "sub"))
    values = jnp.where(got_code >= 0, answer[jnp.clip(got_code, 0, rows_dev - 1)], 0.0)
    homeward = lax.all_to_all(values, "rows", split_axis=0, concat_axis=0, tiled=True)
    return homeward[owner, order]


def normalised(rows):
    wide = rows.astype(jnp.float32)
    squares = jnp.sum(wide * wide, axis=1, keepdims=True)
    return (wide * (1.0 / jnp.sqrt(squares + 1e-06))).astype(jnp.bfloat16)


def unit_kernel(rows_ref, unit_ref):
    unit_ref[...] = normalised(rows_ref[...])


def unit_rows(rows):
    count, width = rows.shape
    step = min(count, 1024)
    return pl.pallas_call(
        unit_kernel,
        grid=(count // step,),
        in_specs=[pl.BlockSpec((step, width), lambda i: (i, 0))],
        out_specs=pl.BlockSpec((step, width), lambda i: (i, 0)),
        out_shape=jax.ShapeDtypeStruct(rows.shape, jnp.bfloat16),
        cost_estimate=pl.CostEstimate(
            flops=4 * count * width, bytes_accessed=4 * count * width, transcendentals=count
        ),
    )(rows)


def tags_kernel(clusters, cores, place_ref, list_ref, slot_ref, *refs):
    passed_refs, (home_ref, own_ref, left_ref, across_ref) = refs[:-4], refs[-4:]
    which, receives = place_ref[0], place_ref[1]
    half = list_ref.shape[0]
    band = own_ref.shape[0]

    def arrived(piece, rows):
        value = passed_refs[0][rows, :]
        for flip in range(1, len(passed_refs)):
            value = jnp.where(which == piece ^ flip, passed_refs[flip][rows, :], value)
        return value

    lists = [list_ref[...]]
    lists += [arrived(piece, pl.ds(0, half)) for piece in (0, cores)] + [arrived(0, pl.ds(2 * half, half))]
    starts = [jnp.sum(sum((ids < k).astype(jnp.int32) for ids in lists)) for k in range(1, clusters)]

    def tags_of(positions):
        return sum((positions >= start).astype(jnp.int32) for start in starts)

    def column(tags):
        return jnp.broadcast_to(tags, (LANES, band)).T

    slots = pl.ds(half + which, 1)
    for row in range(half):
        home_ref[:, pl.ds(row * band, band)] = tags_of(slot_ref[pl.ds(row, 1), :])
    own_ref[...] = column(tags_of(slot_ref[pl.ds(which, 1), :]))
    left_ref[...] = column(tags_of(arrived(0, slots)))
    across_ref[...] = column(jnp.where(receives == 1, tags_of(arrived(cores, slots)), -1))


def tags_for(clusters, cores, which, receives, list_id, slot, passed):
    half, band = list_id.shape
    vmem = pl.BlockSpec(memory_space=pltpu.VMEM)
    columns = jax.ShapeDtypeStruct((band, LANES), jnp.int32)
    total = half * band
    return pl.pallas_call(
        functools.partial(tags_kernel, clusters, cores),
        in_specs=[pl.BlockSpec(memory_space=pltpu.SMEM)] + [vmem] * (2 + len(passed)),
        out_specs=[vmem] * 4,
        out_shape=[jax.ShapeDtypeStruct((1, total), jnp.int32)] + [columns] * 3,
        cost_estimate=pl.CostEstimate(flops=total * 32, bytes_accessed=total * 32, transcendentals=0),
    )(jnp.stack([which, receives.astype(jnp.int32)]), list_id, slot, *passed)


def meet_kernel(same, ready, offset, extra, which_ref, best_ref, home_ref, home_tags_ref, tags_ref, *refs):
    other_refs, (home_best_ref, other_best_ref) = refs[: -2 - extra], refs[-2:]
    homes = home_ref.shape[0]
    unit = jnp.concatenate([ref[...] if ready else normalised(ref[...]) for ref in other_refs])
    others = unit.shape[0]
    tags = tags_ref[pl.ds(offset, others), :1]
    folded = jnp.full((others, LANES), -1.0, jnp.float32)
    if same:
        place = which_ref[0] * others + lax.broadcasted_iota(jnp.int32, (others, TILE), 0)
    for start in range(0, homes, TILE):
        here = pl.ds(start, TILE)
        scores = lax.dot_general(
            unit, home_ref[here, :], (((1,), (1,)), ((), ())), preferred_element_type=jnp.float32
        )
        keep = tags == home_tags_ref[:, here]
        if same:
            keep &= place != start + lax.broadcasted_iota(jnp.int32, (others, TILE), 1)
        scores = jnp.where(keep, scores, -1.0)
        home_best_ref[:, here] = jnp.maximum(best_ref[:, here], jnp.max(scores, axis=0, keepdims=True))
        for lane in range(0, TILE, LANES):
            folded = jnp.maximum(folded, scores[:, lane : lane + LANES])
    if extra:
        other_best_ref[:, :offset] = refs[len(other_refs)][...]
    other_best_ref[:, offset if extra else 0 :] = jnp.max(folded.T, axis=0, keepdims=True)


def meet(others, tags, homes, home_tags, best, which, same=False, ready=False, offset=0, before=None):
    count = sum(rows.shape[0] for rows in others)
    total, width = homes.shape
    before = [] if before is None else [before]
    vmem = pl.BlockSpec(memory_space=pltpu.VMEM)
    return pl.pallas_call(
        functools.partial(meet_kernel, same, ready, offset, len(before)),
        in_specs=[pl.BlockSpec(memory_space=pltpu.SMEM)] + [vmem] * (4 + len(others) + len(before)),
        out_specs=[vmem, vmem],
        out_shape=[
            jax.ShapeDtypeStruct((1, total), jnp.float32),
            jax.ShapeDtypeStruct((1, count + (offset if before else 0)), jnp.float32),
        ],
        compiler_params=pltpu.CompilerParams(vmem_limit_bytes=32 * 1024 * 1024),
        cost_estimate=pl.CostEstimate(
            flops=2 * count * total * width,
            bytes_accessed=2 * (count + total) * width,
            transcendentals=count,
        ),
    )(which.reshape(1), best, homes, home_tags, tags, *others, *before)


def dense(embeddings, slot, list_id):
    rows_dev = embeddings.shape[0]
    peers = lax.axis_size("rows")
    me = lax.axis_index("rows")
    pieces = lax.axis_size(("pairs", "sub"))
    which = lax.axis_index(("pairs", "sub"))
    band = rows_dev // pieces
    half = band // 2
    clusters = peers * rows_dev // POSITIONS_PER_CLUSTER
    round_moves = [(i, (i + 1) % peers) for i in range(peers)]
    across_moves = [(0, 2), (3, 1)]
    receives = (me == 1) | (me == 2)

    cores = lax.axis_size("sub")
    chips = pieces // cores

    def pieces_of(rows, length):
        return rows.reshape(-1, length, rows.shape[1])

    def handed(value, turns):
        moves = [
            (i * pieces + p, (i + turn) % peers * pieces + p) for i in range(peers) for p, turn in turns.items()
        ]
        return lax.ppermute(value, ("rows", "pairs", "sub"), moves)

    message = jnp.concatenate([list_id, slot])
    passed = jnp.concatenate([handed(message, {0: 1, cores: 2}), handed(message, {0: peers - 1})])
    quarter = lax.dynamic_index_in_dim(pieces_of(embeddings, band), which, 0, keepdims=False)
    quarter, embeddings, passed = lax.optimization_barrier((quarter, embeddings, passed))
    round_rows = lax.ppermute(quarter, "rows", round_moves)
    passed = [passed] + [
        lax.ppermute(passed, ("pairs", "sub"), [(p, p ^ flip) for p in range(pieces)])
        for flip in range(1, pieces)
    ]

    homes = unit_rows(embeddings)
    halves = pieces_of(homes, half)
    third, fourth = (
        lax.ppermute(
            lax.dynamic_index_in_dim(halves, 2 * which + i, 0, keepdims=False), "rows", across_moves
        )
        for i in range(2)
    )
    home_tags, own_tags, round_tags, across_tags = tags_for(
        clusters,
        cores,
        which,
        receives,
        list_id.reshape(pieces, band),
        slot.reshape(pieces, band),
        [value.reshape(-1, band) for value in passed],
    )

    best = jnp.full((1, rows_dev), -1.0, jnp.float32)
    best, _ = meet([quarter], own_tags, homes, home_tags, best, which, same=True)
    best, round_best = meet([round_rows], round_tags, homes, home_tags, best, which)
    best, early = meet([third], across_tags, homes, home_tags, best, which, ready=True)
    round_best, best = lax.optimization_barrier((round_best, best))
    round_best = lax.ppermute(round_best, "rows", [(b, a) for a, b in round_moves])
    best, across_best = meet(
        [fourth], across_tags, homes, home_tags, best, which, ready=True, offset=half, before=early
    )

    across_best = lax.ppermute(across_best, "rows", [(b, a) for a, b in across_moves])
    back = jnp.maximum(round_best, jnp.where(receives, -1.0, across_best))
    here = lax.dynamic_slice_in_dim(best, which * band, band, 1)
    best = lax.dynamic_update_slice_in_dim(best, jnp.maximum(here, back), which * band, 1)
    best = jnp.maximum(best, lax.ppermute(best, "pairs", [(i, chips - 1 - i) for i in range(chips)]))
    best = jnp.maximum(best, lax.ppermute(best, "sub", [(i, cores - 1 - i) for i in range(cores)]))
    return best.reshape(rows_dev)


def on_device(embeddings, slot, list_id):
    if lax.axis_size("rows") == SPAN:
        return dense(embeddings, slot, list_id)
    return banded(embeddings, slot, list_id)


def solution(mesh):
    return jax.shard_map(
        on_device,
        mesh=mesh,
        in_specs=(P(("groups", "rows"), None), P(("groups", "rows")), P(("groups", "rows"))),
        out_specs=P(("groups", "rows")),
        check_vma=False,
    )
```

```python
import functools

import jax
import jax.numpy as jnp
from jax import lax
from jax.experimental import pallas as pl
from jax.experimental.pallas import tpu as pltpu
from jax.sharding import PartitionSpec as P

SPAN = 4
POSITIONS_PER_CLUSTER = 1024
LANES = 128
TILE = 256
VMEM_BYTES = 32 * 1024 * 1024


def shifted(value, axis, by):
    length = lax.axis_size(axis)
    pairs = [(i, i + by) for i in range(length) if 0 <= i + by < length]
    return lax.ppermute(value, axis, pairs)


def placed(received, codes, rows_dev):
    flat = received.reshape(-1, received.shape[-1])
    flat_codes = codes.reshape(-1)
    target = jnp.where(flat_codes >= 0, flat_codes, rows_dev)
    return jnp.zeros((rows_dev, flat.shape[1]), flat.dtype).at[target].set(flat, mode="drop")


def masked_scores(owned, tags, far_rows, far_tags):
    scores = lax.dot_general(
        owned, far_rows, (((1,), (1,)), ((), ())), preferred_element_type=jnp.float32
    )
    return jnp.where(tags[:, None] == far_tags[None, :], scores, -1.0)


def banded(embeddings, slot, list_id):
    rows_dev = embeddings.shape[0]
    width = embeddings.shape[1]
    peers = lax.axis_size("rows")
    capacity = 3 * (rows_dev // peers) // 2
    wide = embeddings.astype(jnp.float32)
    unit = (wide / jnp.sqrt(jnp.sum(wide * wide, axis=1, keepdims=True) + 1e-06)).astype(
        jnp.bfloat16
    )
    owner = slot // rows_dev
    local = slot - owner * rows_dev
    onehot = (owner[:, None] == jnp.arange(peers, dtype=jnp.int32)[None, :]).astype(jnp.int32)
    order = jnp.sum((jnp.cumsum(onehot, axis=0) - onehot) * onehot, axis=1)
    send_code = jnp.full((peers, capacity), -1, jnp.int32).at[owner, order].set(local)
    pieces = lax.axis_size(("pairs", "sub"))
    which = lax.axis_index(("pairs", "sub"))
    send_rows = jnp.zeros((peers, capacity, width), jnp.bfloat16).at[owner, order].set(unit)
    got_rows, got_code = (
        lax.all_to_all(send_rows, "rows", split_axis=0, concat_axis=0, tiled=True),
        lax.all_to_all(send_code, "rows", split_axis=0, concat_axis=0, tiled=True),
    )
    owned = placed(got_rows, got_code, rows_dev)
    tags = list_id + 1
    band = rows_dev // pieces
    columns = lax.dynamic_slice_in_dim(owned, which * band, band, 0)
    column_tags = lax.dynamic_slice_in_dim(tags, which * band, band, 0)
    row_index = jnp.arange(rows_dev, dtype=jnp.int32)
    column_index = which * band + jnp.arange(band, dtype=jnp.int32)
    near = masked_scores(owned, tags, columns, column_tags)
    near = jnp.where(row_index[:, None] == column_index[None, :], -1.0, near)
    best = jnp.max(near, axis=1)
    offsets = list(range(1 - SPAN, 0)) + list(range(1, SPAN))
    for step in offsets:
        far_rows, far_tags = shifted((columns, column_tags), "rows", step)
        best = jnp.maximum(best, jnp.max(masked_scores(owned, tags, far_rows, far_tags), axis=1))
    answer = lax.pmax(best, ("pairs", "sub"))
    values = jnp.where(got_code >= 0, answer[jnp.clip(got_code, 0, rows_dev - 1)], 0.0)
    homeward = lax.all_to_all(values, "rows", split_axis=0, concat_axis=0, tiled=True)
    return homeward[owner, order]


def normalised(rows):
    wide = rows.astype(jnp.float32)
    squares = jnp.sum(wide * wide, axis=1, keepdims=True)
    return (wide * (1.0 / jnp.sqrt(squares + 1e-06))).astype(jnp.bfloat16)


def unit_kernel(rows_ref, unit_ref):
    unit_ref[...] = normalised(rows_ref[...])


def unit_rows(rows):
    count, width = rows.shape
    step = min(count, 1024)
    return pl.pallas_call(
        unit_kernel,
        grid=(count // step,),
        in_specs=[pl.BlockSpec((step, width), lambda i: (i, 0))],
        out_specs=pl.BlockSpec((step, width), lambda i: (i, 0)),
        out_shape=jax.ShapeDtypeStruct(rows.shape, jnp.bfloat16),
        cost_estimate=pl.CostEstimate(
            flops=4 * count * width, bytes_accessed=4 * count * width, transcendentals=count
        ),
    )(rows)


def tags_kernel(clusters, place_ref, list_ref, slot_ref, *refs):
    passed_refs, (home_ref, own_ref, left_ref, across_ref) = refs[:-4], refs[-4:]
    which, odd, receives = place_ref[0], place_ref[1] == 1, place_ref[2] == 1
    total = list_ref.shape[1]
    band = own_ref.shape[0]

    def arrived(piece, lanes):
        value = passed_refs[0][:, lanes]
        for flip in range(1, len(passed_refs)):
            value = jnp.where(which == piece ^ flip, passed_refs[flip][:, lanes], value)
        return value

    lists = [list_ref[...]] + [arrived(piece, pl.ds(0, total)) for piece in range(len(passed_refs) - 1)]
    lists = jnp.concatenate([ids[:, i : i + LANES] for ids in lists for i in range(0, total, LANES)])
    starts = [jnp.sum((lists < k).astype(jnp.int32)) for k in range(1, clusters)]

    def tags_of(positions):
        return sum((positions >= start).astype(jnp.int32) for start in starts)

    def column(tags):
        return jnp.broadcast_to(tags, (LANES, band)).T

    mine = pl.multiple_of(which * band, band)
    slots = pl.ds(total + mine, band)
    home_ref[...] = tags_of(slot_ref[...])
    own_ref[...] = column(tags_of(slot_ref[:, pl.ds(mine, band)]))
    left_ref[...] = column(tags_of(jnp.where(odd, arrived(0, slots), arrived(2, slots))))
    across_ref[...] = column(jnp.where(receives, tags_of(arrived(1, slots)), -1))


def tags_for(clusters, place, band, list_id, slot, passed):
    vmem = pl.BlockSpec(memory_space=pltpu.VMEM)
    columns = jax.ShapeDtypeStruct((band, LANES), jnp.int32)
    total = slot.shape[1]
    return pl.pallas_call(
        functools.partial(tags_kernel, clusters),
        in_specs=[pl.BlockSpec(memory_space=pltpu.SMEM)] + [vmem] * (2 + len(passed)),
        out_specs=[vmem] * 4,
        out_shape=[jax.ShapeDtypeStruct((1, total), jnp.int32)] + [columns] * 3,
        cost_estimate=pl.CostEstimate(flops=total * 32, bytes_accessed=total * 32, transcendentals=0),
    )(place, list_id, slot, *passed)


def meet_kernel(same, ready, offset, extra, which_ref, best_ref, home_ref, home_tags_ref, tags_ref, *refs):
    other_refs, (home_best_ref, other_best_ref) = refs[: -2 - extra], refs[-2:]
    homes = home_ref.shape[0]
    unit = jnp.concatenate([ref[...] if ready else normalised(ref[...]) for ref in other_refs])
    others = unit.shape[0]
    tags = tags_ref[pl.ds(offset, others), :1]
    folded = jnp.full((others, LANES), -1.0, jnp.float32)
    if same:
        place = which_ref[0] * others + lax.broadcasted_iota(jnp.int32, (others, TILE), 0)
    for start in range(0, homes, TILE):
        here = pl.ds(start, TILE)
        scores = lax.dot_general(
            unit, home_ref[here, :], (((1,), (1,)), ((), ())), preferred_element_type=jnp.float32
        )
        keep = tags == home_tags_ref[:, here]
        if same:
            keep &= place != start + lax.broadcasted_iota(jnp.int32, (others, TILE), 1)
        scores = jnp.where(keep, scores, -1.0)
        home_best_ref[:, here] = jnp.maximum(best_ref[:, here], jnp.max(scores, axis=0, keepdims=True))
        for lane in range(0, TILE, LANES):
            folded = jnp.maximum(folded, scores[:, lane : lane + LANES])
    if extra:
        other_best_ref[:, :offset] = refs[len(other_refs)][...]
    other_best_ref[:, offset if extra else 0 :] = jnp.max(folded.T, axis=0, keepdims=True)


def meet(others, tags, homes, home_tags, best, which, same=False, ready=False, offset=0, before=None):
    count = sum(rows.shape[0] for rows in others)
    total, width = homes.shape
    before = [] if before is None else [before]
    vmem = pl.BlockSpec(memory_space=pltpu.VMEM)
    return pl.pallas_call(
        functools.partial(meet_kernel, same, ready, offset, len(before)),
        in_specs=[pl.BlockSpec(memory_space=pltpu.SMEM)] + [vmem] * (4 + len(others) + len(before)),
        out_specs=[vmem, vmem],
        out_shape=[
            jax.ShapeDtypeStruct((1, total), jnp.float32),
            jax.ShapeDtypeStruct((1, count + (offset if before else 0)), jnp.float32),
        ],
        compiler_params=pltpu.CompilerParams(vmem_limit_bytes=VMEM_BYTES),
        cost_estimate=pl.CostEstimate(
            flops=2 * count * total * width,
            bytes_accessed=2 * (count + total) * width,
            transcendentals=count,
        ),
    )(which.reshape(1), best, homes, home_tags, tags, *others, *before)


def dense(embeddings, slot, list_id):
    rows_dev = embeddings.shape[0]
    peers = lax.axis_size("rows")
    me = lax.axis_index("rows")
    pieces = lax.axis_size(("pairs", "sub"))
    which = lax.axis_index(("pairs", "sub"))
    band = rows_dev // pieces
    half = band // 2
    clusters = peers * rows_dev // POSITIONS_PER_CLUSTER
    round_moves = [(i, (i + 1) % peers) for i in range(peers)]
    across_moves = [(0, 2), (3, 1)]
    receives = (me == 1) | (me == 2)

    cores = lax.axis_size("sub")
    chips = pieces // cores

    def pieces_of(rows, length):
        return rows.reshape(-1, length, rows.shape[1])

    passed = lax.ppermute(
        jnp.concatenate([list_id, slot]),
        ("rows", "pairs", "sub"),
        [(i * pieces + p, (i ^ ((1, 2, 3, 3)[p])) * pieces + p) for i in range(peers) for p in range(peers)],
    )
    quarter = lax.dynamic_index_in_dim(pieces_of(embeddings, band), which, 0, keepdims=False)
    quarter, embeddings, passed = lax.optimization_barrier((quarter, embeddings, passed))
    round_rows = lax.ppermute(quarter, "rows", round_moves)
    passed = [passed] + [
        lax.ppermute(passed, ("pairs", "sub"), [(p, p ^ flip) for p in range(pieces)])
        for flip in range(1, pieces)
    ]

    homes = unit_rows(embeddings)
    halves = pieces_of(homes, half)
    third, fourth = (
        lax.ppermute(
            lax.dynamic_index_in_dim(halves, 2 * which + i, 0, keepdims=False), "rows", across_moves
        )
        for i in range(2)
    )
    home_tags, own_tags, round_tags, across_tags = tags_for(
        clusters,
        jnp.stack([which, me % 2, receives.astype(jnp.int32)]),
        band,
        list_id[None],
        slot[None],
        [value[None] for value in passed],
    )

    best = jnp.full((1, rows_dev), -1.0, jnp.float32)
    best, _ = meet([quarter], own_tags, homes, home_tags, best, which, same=True)
    best, round_best = meet([round_rows], round_tags, homes, home_tags, best, which)
    best, early = meet([third], across_tags, homes, home_tags, best, which, ready=True)
    round_best, best = lax.optimization_barrier((round_best, best))
    round_best = lax.ppermute(
        jnp.broadcast_to(round_best, (8, band)), "rows", [(b, a) for a, b in round_moves]
    )[:1]
    best, across_best = meet(
        [fourth], across_tags, homes, home_tags, best, which, ready=True, offset=half, before=early
    )

    across_best = lax.ppermute(across_best, "rows", [(b, a) for a, b in across_moves])
    back = jnp.maximum(round_best, jnp.where(receives, -1.0, across_best))
    here = lax.dynamic_slice_in_dim(best, which * band, band, 1)
    best = lax.dynamic_update_slice_in_dim(best, jnp.maximum(here, back), which * band, 1)
    best = jnp.maximum(best, lax.ppermute(best, "pairs", [(i, chips - 1 - i) for i in range(chips)]))
    best = jnp.maximum(best, lax.ppermute(best, "sub", [(i, cores - 1 - i) for i in range(cores)]))
    return best.reshape(rows_dev)


def on_device(embeddings, slot, list_id):
    if lax.axis_size("rows") == SPAN:
        return dense(embeddings, slot, list_id)
    return banded(embeddings, slot, list_id)


def solution(mesh):
    return jax.shard_map(
        on_device,
        mesh=mesh,
        in_specs=(P(("groups", "rows"), None), P(("groups", "rows")), P(("groups", "rows"))),
        out_specs=P(("groups", "rows")),
        check_vma=False,
    )
```

```python
import functools

import jax
import jax.numpy as jnp
from jax import lax
from jax.experimental import pallas as pl
from jax.experimental.pallas import tpu as pltpu
from jax.sharding import PartitionSpec as P

SPAN = 4
POSITIONS_PER_CLUSTER = 1024
LANES = 128
TILE = 256
VMEM_BYTES = 32 * 1024 * 1024


def shifted(value, axis, by):
    length = lax.axis_size(axis)
    pairs = [(i, i + by) for i in range(length) if 0 <= i + by < length]
    return lax.ppermute(value, axis, pairs)


def placed(received, codes, rows_dev):
    flat = received.reshape(-1, received.shape[-1])
    flat_codes = codes.reshape(-1)
    target = jnp.where(flat_codes >= 0, flat_codes, rows_dev)
    return jnp.zeros((rows_dev, flat.shape[1]), flat.dtype).at[target].set(flat, mode="drop")


def masked_scores(owned, tags, far_rows, far_tags):
    scores = lax.dot_general(
        owned, far_rows, (((1,), (1,)), ((), ())), preferred_element_type=jnp.float32
    )
    return jnp.where(tags[:, None] == far_tags[None, :], scores, -1.0)


def banded(embeddings, slot, list_id):
    rows_dev = embeddings.shape[0]
    width = embeddings.shape[1]
    peers = lax.axis_size("rows")
    capacity = 3 * (rows_dev // peers) // 2
    wide = embeddings.astype(jnp.float32)
    unit = (wide / jnp.sqrt(jnp.sum(wide * wide, axis=1, keepdims=True) + 1e-06)).astype(
        jnp.bfloat16
    )
    owner = slot // rows_dev
    local = slot - owner * rows_dev
    onehot = (owner[:, None] == jnp.arange(peers, dtype=jnp.int32)[None, :]).astype(jnp.int32)
    order = jnp.sum((jnp.cumsum(onehot, axis=0) - onehot) * onehot, axis=1)
    send_code = jnp.full((peers, capacity), -1, jnp.int32).at[owner, order].set(local)
    pieces = lax.axis_size(("pairs", "sub"))
    which = lax.axis_index(("pairs", "sub"))
    send_rows = jnp.zeros((peers, capacity, width), jnp.bfloat16).at[owner, order].set(unit)
    got_rows, got_code = (
        lax.all_to_all(send_rows, "rows", split_axis=0, concat_axis=0, tiled=True),
        lax.all_to_all(send_code, "rows", split_axis=0, concat_axis=0, tiled=True),
    )
    owned = placed(got_rows, got_code, rows_dev)
    tags = list_id + 1
    band = rows_dev // pieces
    columns = lax.dynamic_slice_in_dim(owned, which * band, band, 0)
    column_tags = lax.dynamic_slice_in_dim(tags, which * band, band, 0)
    row_index = jnp.arange(rows_dev, dtype=jnp.int32)
    column_index = which * band + jnp.arange(band, dtype=jnp.int32)
    near = masked_scores(owned, tags, columns, column_tags)
    near = jnp.where(row_index[:, None] == column_index[None, :], -1.0, near)
    best = jnp.max(near, axis=1)
    offsets = list(range(1 - SPAN, 0)) + list(range(1, SPAN))
    for step in offsets:
        far_rows, far_tags = shifted((columns, column_tags), "rows", step)
        best = jnp.maximum(best, jnp.max(masked_scores(owned, tags, far_rows, far_tags), axis=1))
    answer = lax.pmax(best, ("pairs", "sub"))
    values = jnp.where(got_code >= 0, answer[jnp.clip(got_code, 0, rows_dev - 1)], 0.0)
    homeward = lax.all_to_all(values, "rows", split_axis=0, concat_axis=0, tiled=True)
    return homeward[owner, order]


def normalised(rows):
    wide = rows.astype(jnp.float32)
    squares = jnp.sum(wide * wide, axis=1, keepdims=True)
    return (wide * (1.0 / jnp.sqrt(squares + 1e-06))).astype(jnp.bfloat16)


def unit_kernel(rows_ref, unit_ref):
    unit_ref[...] = normalised(rows_ref[...])


def unit_rows(rows):
    count, width = rows.shape
    step = min(count, 1024)
    return pl.pallas_call(
        unit_kernel,
        grid=(count // step,),
        in_specs=[pl.BlockSpec((step, width), lambda i: (i, 0))],
        out_specs=pl.BlockSpec((step, width), lambda i: (i, 0)),
        out_shape=jax.ShapeDtypeStruct(rows.shape, jnp.bfloat16),
        cost_estimate=pl.CostEstimate(
            flops=4 * count * width, bytes_accessed=4 * count * width, transcendentals=count
        ),
    )(rows)


def tags_kernel(clusters, place_ref, list_ref, slot_ref, *refs):
    passed_refs, (home_ref, own_ref, left_ref, across_ref) = refs[:-4], refs[-4:]
    which, odd, receives = place_ref[0], place_ref[1] == 1, place_ref[2] == 1
    total = list_ref.shape[1]
    band = own_ref.shape[0]

    def arrived(piece, lanes):
        value = passed_refs[0][:, lanes]
        for flip in range(1, len(passed_refs)):
            value = jnp.where(which == piece ^ flip, passed_refs[flip][:, lanes], value)
        return value

    lists = [list_ref[...]] + [arrived(piece, pl.ds(0, total)) for piece in range(len(passed_refs) - 1)]
    lists = jnp.concatenate([ids[:, i : i + LANES] for ids in lists for i in range(0, total, LANES)])
    starts = [jnp.sum((lists < k).astype(jnp.int32)) for k in range(1, clusters)]

    def tags_of(positions):
        return sum((positions >= start).astype(jnp.int32) for start in starts)

    def column(tags):
        return jnp.broadcast_to(tags, (LANES, band)).T

    mine = pl.multiple_of(which * band, band)
    slots = pl.ds(total + mine, band)
    home_ref[...] = tags_of(slot_ref[...])
    own_ref[...] = column(tags_of(slot_ref[:, pl.ds(mine, band)]))
    left_ref[...] = column(tags_of(jnp.where(odd, arrived(0, slots), arrived(2, slots))))
    across_ref[...] = column(jnp.where(receives, tags_of(arrived(1, slots)), -1))


def tags_for(clusters, place, band, list_id, slot, passed):
    vmem = pl.BlockSpec(memory_space=pltpu.VMEM)
    columns = jax.ShapeDtypeStruct((band, LANES), jnp.int32)
    total = slot.shape[1]
    return pl.pallas_call(
        functools.partial(tags_kernel, clusters),
        in_specs=[pl.BlockSpec(memory_space=pltpu.SMEM)] + [vmem] * (2 + len(passed)),
        out_specs=[vmem] * 4,
        out_shape=[jax.ShapeDtypeStruct((1, total), jnp.int32)] + [columns] * 3,
        cost_estimate=pl.CostEstimate(flops=total * 32, bytes_accessed=total * 32, transcendentals=0),
    )(place, list_id, slot, *passed)


def meet_kernel(same, ready, offset, extra, which_ref, best_ref, home_ref, home_tags_ref, tags_ref, *refs):
    other_refs, (home_best_ref, other_best_ref) = refs[: -2 - extra], refs[-2:]
    homes = home_ref.shape[0]
    unit = jnp.concatenate([ref[...] if ready else normalised(ref[...]) for ref in other_refs])
    others = unit.shape[0]
    tags = tags_ref[pl.ds(offset, others), :1]
    folded = jnp.full((others, LANES), -1.0, jnp.float32)
    if same:
        place = which_ref[0] * others + lax.broadcasted_iota(jnp.int32, (others, TILE), 0)
    for start in range(0, homes, TILE):
        here = pl.ds(start, TILE)
        scores = lax.dot_general(
            unit, home_ref[here, :], (((1,), (1,)), ((), ())), preferred_element_type=jnp.float32
        )
        keep = tags == home_tags_ref[:, here]
        if same:
            keep &= place != start + lax.broadcasted_iota(jnp.int32, (others, TILE), 1)
        scores = jnp.where(keep, scores, -1.0)
        home_best_ref[:, here] = jnp.maximum(best_ref[:, here], jnp.max(scores, axis=0, keepdims=True))
        for lane in range(0, TILE, LANES):
            folded = jnp.maximum(folded, scores[:, lane : lane + LANES])
    if extra:
        other_best_ref[:, :offset] = refs[len(other_refs)][...]
    other_best_ref[:, offset if extra else 0 :] = jnp.max(folded.T, axis=0, keepdims=True)


def meet(others, tags, homes, home_tags, best, which, same=False, ready=False, offset=0, before=None):
    count = sum(rows.shape[0] for rows in others)
    total, width = homes.shape
    before = [] if before is None else [before]
    vmem = pl.BlockSpec(memory_space=pltpu.VMEM)
    return pl.pallas_call(
        functools.partial(meet_kernel, same, ready, offset, len(before)),
        in_specs=[pl.BlockSpec(memory_space=pltpu.SMEM)] + [vmem] * (4 + len(others) + len(before)),
        out_specs=[vmem, vmem],
        out_shape=[
            jax.ShapeDtypeStruct((1, total), jnp.float32),
            jax.ShapeDtypeStruct((1, count + (offset if before else 0)), jnp.float32),
        ],
        compiler_params=pltpu.CompilerParams(vmem_limit_bytes=VMEM_BYTES),
        cost_estimate=pl.CostEstimate(
            flops=2 * count * total * width,
            bytes_accessed=2 * (count + total) * width,
            transcendentals=count,
        ),
    )(which.reshape(1), best, homes, home_tags, tags, *others, *before)


def dense(embeddings, slot, list_id):
    rows_dev = embeddings.shape[0]
    peers = lax.axis_size("rows")
    me = lax.axis_index("rows")
    pieces = lax.axis_size(("pairs", "sub"))
    which = lax.axis_index(("pairs", "sub"))
    band = rows_dev // pieces
    half = band // 2
    clusters = peers * rows_dev // POSITIONS_PER_CLUSTER
    round_moves = [(i, (i + 1) % peers) for i in range(peers)]
    across_moves = [(0, 2), (3, 1)]
    receives = (me == 1) | (me == 2)

    cores = lax.axis_size("sub")
    chips = pieces // cores

    def pieces_of(rows, length):
        return rows.reshape(-1, length, rows.shape[1])

    passed = lax.ppermute(
        jnp.concatenate([list_id, slot]),
        ("rows", "pairs", "sub"),
        [(i * pieces + p, (i ^ ((1, 2, 3, 3)[p])) * pieces + p) for i in range(peers) for p in range(peers)],
    )
    quarter = lax.dynamic_index_in_dim(pieces_of(embeddings, band), which, 0, keepdims=False)
    quarter, embeddings, passed = lax.optimization_barrier((quarter, embeddings, passed))
    round_rows = lax.ppermute(quarter, "rows", round_moves)
    passed = [passed] + [
        lax.ppermute(passed, ("pairs", "sub"), [(p, p ^ flip) for p in range(pieces)])
        for flip in range(1, pieces)
    ]

    homes = unit_rows(embeddings)
    halves = pieces_of(homes, half)
    third, fourth = (
        lax.ppermute(
            lax.dynamic_index_in_dim(halves, 2 * which + i, 0, keepdims=False), "rows", across_moves
        )
        for i in range(2)
    )
    home_tags, own_tags, round_tags, across_tags = tags_for(
        clusters,
        jnp.stack([which, me % 2, receives.astype(jnp.int32)]),
        band,
        list_id[None],
        slot[None],
        [value[None] for value in passed],
    )

    best = jnp.full((1, rows_dev), -1.0, jnp.float32)
    best, _ = meet([quarter], own_tags, homes, home_tags, best, which, same=True)
    best, round_best = meet([round_rows], round_tags, homes, home_tags, best, which)
    best, early = meet([third], across_tags, homes, home_tags, best, which, ready=True)
    round_best, best = lax.optimization_barrier((round_best, best))
    round_best = lax.ppermute(round_best, "rows", [(b, a) for a, b in round_moves])
    round_best, best = lax.optimization_barrier((round_best, best))
    best, across_best = meet(
        [fourth], across_tags, homes, home_tags, best, which, ready=True, offset=half, before=early
    )

    chip, core = lax.axis_index("pairs"), lax.axis_index("sub")
    swap_cores = [(i, cores - 1 - i) for i in range(cores)]
    shared = lax.ppermute(across_best, "sub", swap_cores)
    shared = jnp.concatenate(
        [jnp.where(core == 0, across_best, shared), jnp.where(core == 0, shared, across_best)], axis=1
    )
    here = lax.dynamic_slice_in_dim(best, which * band, band, 1)
    best = lax.dynamic_update_slice_in_dim(best, jnp.maximum(here, round_best), which * band, 1)
    back = lax.ppermute(
        jnp.broadcast_to(shared, (4, cores * band)),
        ("rows", "pairs", "sub"),
        [
            ((b * chips + x) * cores + c, (a * chips + (x ^ c)) * cores + c)
            for a, b in across_moves
            for x in range(chips)
            for c in range(cores)
        ],
    )[:1]
    back = jnp.where(receives, -1.0, back)
    swapped = lax.ppermute(best, "pairs", [(i, chips - 1 - i) for i in range(chips)])
    first = (chip ^ core) * cores * band
    here = lax.dynamic_slice_in_dim(best, first, cores * band, 1)
    best = lax.dynamic_update_slice_in_dim(best, jnp.maximum(here, back), first, 1)
    best = jnp.maximum(best, swapped)
    best = jnp.maximum(best, lax.ppermute(best, "sub", swap_cores))
    return best.reshape(rows_dev)


def on_device(embeddings, slot, list_id):
    if lax.axis_size("rows") == SPAN:
        return dense(embeddings, slot, list_id)
    return banded(embeddings, slot, list_id)


def solution(mesh):
    return jax.shard_map(
        on_device,
        mesh=mesh,
        in_specs=(P(("groups", "rows"), None), P(("groups", "rows")), P(("groups", "rows"))),
        out_specs=P(("groups", "rows")),
        check_vma=False,
    )
```

```python
import functools

import jax
import jax.numpy as jnp
from jax import lax
from jax.experimental import pallas as pl
from jax.experimental.pallas import tpu as pltpu
from jax.sharding import PartitionSpec as P

SPAN = 4
POSITIONS_PER_CLUSTER = 1024
LANES = 128
TILE = 256
VMEM_BYTES = 32 * 1024 * 1024


def shifted(value, axis, by):
    length = lax.axis_size(axis)
    pairs = [(i, i + by) for i in range(length) if 0 <= i + by < length]
    return lax.ppermute(value, axis, pairs)


def placed(received, codes, rows_dev):
    flat = received.reshape(-1, received.shape[-1])
    flat_codes = codes.reshape(-1)
    target = jnp.where(flat_codes >= 0, flat_codes, rows_dev)
    return jnp.zeros((rows_dev, flat.shape[1]), flat.dtype).at[target].set(flat, mode="drop")


def masked_scores(owned, tags, far_rows, far_tags):
    scores = lax.dot_general(
        owned, far_rows, (((1,), (1,)), ((), ())), preferred_element_type=jnp.float32
    )
    return jnp.where(tags[:, None] == far_tags[None, :], scores, -1.0)


def banded(embeddings, slot, list_id):
    rows_dev = embeddings.shape[0]
    width = embeddings.shape[1]
    peers = lax.axis_size("rows")
    capacity = 3 * (rows_dev // peers) // 2
    wide = embeddings.astype(jnp.float32)
    unit = (wide / jnp.sqrt(jnp.sum(wide * wide, axis=1, keepdims=True) + 1e-06)).astype(
        jnp.bfloat16
    )
    owner = slot // rows_dev
    local = slot - owner * rows_dev
    onehot = (owner[:, None] == jnp.arange(peers, dtype=jnp.int32)[None, :]).astype(jnp.int32)
    order = jnp.sum((jnp.cumsum(onehot, axis=0) - onehot) * onehot, axis=1)
    send_code = jnp.full((peers, capacity), -1, jnp.int32).at[owner, order].set(local)
    pieces = lax.axis_size(("pairs", "sub"))
    which = lax.axis_index(("pairs", "sub"))
    send_rows = jnp.zeros((peers, capacity, width), jnp.bfloat16).at[owner, order].set(unit)
    got_rows, got_code = (
        lax.all_to_all(send_rows, "rows", split_axis=0, concat_axis=0, tiled=True),
        lax.all_to_all(send_code, "rows", split_axis=0, concat_axis=0, tiled=True),
    )
    owned = placed(got_rows, got_code, rows_dev)
    tags = list_id + 1
    band = rows_dev // pieces
    columns = lax.dynamic_slice_in_dim(owned, which * band, band, 0)
    column_tags = lax.dynamic_slice_in_dim(tags, which * band, band, 0)
    row_index = jnp.arange(rows_dev, dtype=jnp.int32)
    column_index = which * band + jnp.arange(band, dtype=jnp.int32)
    near = masked_scores(owned, tags, columns, column_tags)
    near = jnp.where(row_index[:, None] == column_index[None, :], -1.0, near)
    best = jnp.max(near, axis=1)
    offsets = list(range(1 - SPAN, 0)) + list(range(1, SPAN))
    for step in offsets:
        far_rows, far_tags = shifted((columns, column_tags), "rows", step)
        best = jnp.maximum(best, jnp.max(masked_scores(owned, tags, far_rows, far_tags), axis=1))
    answer = lax.pmax(best, ("pairs", "sub"))
    values = jnp.where(got_code >= 0, answer[jnp.clip(got_code, 0, rows_dev - 1)], 0.0)
    homeward = lax.all_to_all(values, "rows", split_axis=0, concat_axis=0, tiled=True)
    return homeward[owner, order]


def normalised(rows):
    wide = rows.astype(jnp.float32)
    squares = jnp.sum(wide * wide, axis=1, keepdims=True)
    return (wide * (1.0 / jnp.sqrt(squares + 1e-06))).astype(jnp.bfloat16)


def unit_kernel(rows_ref, unit_ref):
    unit_ref[...] = normalised(rows_ref[...])


def unit_rows(rows):
    count, width = rows.shape
    step = min(count, 1024)
    return pl.pallas_call(
        unit_kernel,
        grid=(count // step,),
        in_specs=[pl.BlockSpec((step, width), lambda i: (i, 0))],
        out_specs=pl.BlockSpec((step, width), lambda i: (i, 0)),
        out_shape=jax.ShapeDtypeStruct(rows.shape, jnp.bfloat16),
        cost_estimate=pl.CostEstimate(
            flops=4 * count * width, bytes_accessed=4 * count * width, transcendentals=count
        ),
    )(rows)


def tags_kernel(clusters, place_ref, list_ref, slot_ref, *refs):
    passed_refs, (home_ref, own_ref, left_ref, across_ref) = refs[:-4], refs[-4:]
    which, odd, receives = place_ref[0], place_ref[1] == 1, place_ref[2] == 1
    total = list_ref.shape[1]
    band = own_ref.shape[0]

    def arrived(piece, lanes):
        value = passed_refs[0][:, lanes]
        for flip in range(1, len(passed_refs)):
            value = jnp.where(which == piece ^ flip, passed_refs[flip][:, lanes], value)
        return value

    lists = [list_ref[...]] + [arrived(piece, pl.ds(0, total)) for piece in range(len(passed_refs) - 1)]
    lists = jnp.concatenate([ids[:, i : i + LANES] for ids in lists for i in range(0, total, LANES)])
    starts = [jnp.sum((lists < k).astype(jnp.int32)) for k in range(1, clusters)]

    def tags_of(positions):
        return sum((positions >= start).astype(jnp.int32) for start in starts)

    def column(tags):
        return jnp.broadcast_to(tags, (LANES, band)).T

    mine = pl.multiple_of(which * band, band)
    slots = pl.ds(total + mine, band)
    home_ref[...] = tags_of(slot_ref[...])
    own_ref[...] = column(tags_of(slot_ref[:, pl.ds(mine, band)]))
    left_ref[...] = column(tags_of(jnp.where(odd, arrived(0, slots), arrived(2, slots))))
    across_ref[...] = column(jnp.where(receives, tags_of(arrived(1, slots)), -1))


def tags_for(clusters, place, band, list_id, slot, passed):
    vmem = pl.BlockSpec(memory_space=pltpu.VMEM)
    columns = jax.ShapeDtypeStruct((band, LANES), jnp.int32)
    total = slot.shape[1]
    return pl.pallas_call(
        functools.partial(tags_kernel, clusters),
        in_specs=[pl.BlockSpec(memory_space=pltpu.SMEM)] + [vmem] * (2 + len(passed)),
        out_specs=[vmem] * 4,
        out_shape=[jax.ShapeDtypeStruct((1, total), jnp.int32)] + [columns] * 3,
        cost_estimate=pl.CostEstimate(flops=total * 32, bytes_accessed=total * 32, transcendentals=0),
    )(place, list_id, slot, *passed)


def meet_rows(same, ready, offset, extra, which_ref, best_ref, home_ref, home_tags_ref, tags_ref, *refs):
    other_refs, (home_best_ref, other_best_ref) = refs[: -2 - extra], refs[-2:]
    homes = home_ref.shape[0]
    unit = jnp.concatenate([ref[...] if ready else normalised(ref[...]) for ref in other_refs])
    others = unit.shape[0]
    tags = tags_ref[pl.ds(offset, others), :1]
    folded = jnp.full((others, LANES), -1.0, jnp.float32)
    if same:
        place = which_ref[0] * others + lax.broadcasted_iota(jnp.int32, (others, TILE), 0)
    for start in range(0, homes, TILE):
        here = pl.ds(start, TILE)
        scores = lax.dot_general(
            unit, home_ref[here, :], (((1,), (1,)), ((), ())), preferred_element_type=jnp.float32
        )
        keep = tags == home_tags_ref[:, here]
        if same:
            keep &= place != start + lax.broadcasted_iota(jnp.int32, (others, TILE), 1)
        scores = jnp.where(keep, scores, -1.0)
        home_best_ref[:, here] = jnp.maximum(best_ref[:, here], jnp.max(scores, axis=0, keepdims=True))
        for lane in range(0, TILE, LANES):
            folded = jnp.maximum(folded, scores[:, lane : lane + LANES])
    if extra:
        other_best_ref[:, :offset] = refs[len(other_refs)][...]
    other_best_ref[:, offset if extra else 0 :] = jnp.max(folded.T, axis=0, keepdims=True)


def meet_kernel(gated, same, ready, offset, extra, flag_ref, best_ref, *refs):
    if not gated:
        meet_rows(same, ready, offset, extra, flag_ref, best_ref, *refs)
        return

    @pl.when(flag_ref[0] == 1)
    def _():
        meet_rows(same, ready, offset, extra, flag_ref, best_ref, *refs)

    @pl.when(flag_ref[0] != 1)
    def _():
        refs[-2][...] = best_ref[...]
        refs[-1][...] = jnp.full(refs[-1].shape, -1.0, jnp.float32)


def meet(others, tags, homes, home_tags, best, flag, same=False, ready=False, offset=0, before=None, gated=False):
    count = sum(rows.shape[0] for rows in others)
    total, width = homes.shape
    before = [] if before is None else [before]
    vmem = pl.BlockSpec(memory_space=pltpu.VMEM)
    return pl.pallas_call(
        functools.partial(meet_kernel, gated, same, ready, offset, len(before)),
        in_specs=[pl.BlockSpec(memory_space=pltpu.SMEM)] + [vmem] * (4 + len(others) + len(before)),
        out_specs=[vmem, vmem],
        out_shape=[
            jax.ShapeDtypeStruct((1, total), jnp.float32),
            jax.ShapeDtypeStruct((1, count + (offset if before else 0)), jnp.float32),
        ],
        compiler_params=pltpu.CompilerParams(vmem_limit_bytes=VMEM_BYTES),
        cost_estimate=pl.CostEstimate(
            flops=2 * count * total * width,
            bytes_accessed=2 * (count + total) * width,
            transcendentals=count,
        ),
    )(flag.reshape(1), best, homes, home_tags, tags, *others, *before)


def dense(embeddings, slot, list_id):
    rows_dev = embeddings.shape[0]
    peers = lax.axis_size("rows")
    me = lax.axis_index("rows")
    pieces = lax.axis_size(("pairs", "sub"))
    which = lax.axis_index(("pairs", "sub"))
    band = rows_dev // pieces
    half = band // 2
    clusters = peers * rows_dev // POSITIONS_PER_CLUSTER
    round_moves = [(i, (i + 1) % peers) for i in range(peers)]
    across_moves = [(0, 2), (3, 1)]
    receives = (me == 1) | (me == 2)

    cores = lax.axis_size("sub")
    chips = pieces // cores

    def pieces_of(rows, length):
        return rows.reshape(-1, length, rows.shape[1])

    passed = lax.ppermute(
        jnp.concatenate([list_id, slot]),
        ("rows", "pairs", "sub"),
        [(i * pieces + p, (i ^ ((1, 2, 3, 3)[p])) * pieces + p) for i in range(peers) for p in range(peers)],
    )
    quarter = lax.dynamic_index_in_dim(pieces_of(embeddings, band), which, 0, keepdims=False)
    quarter, embeddings, passed = lax.optimization_barrier((quarter, embeddings, passed))
    round_rows = lax.ppermute(quarter, "rows", round_moves)
    passed = [passed] + [
        lax.ppermute(passed, ("pairs", "sub"), [(p, p ^ flip) for p in range(pieces)])
        for flip in range(1, pieces)
    ]

    homes = unit_rows(embeddings)
    halves = pieces_of(homes, half)
    third, fourth = (
        lax.ppermute(
            lax.dynamic_index_in_dim(halves, 2 * which + i, 0, keepdims=False), "rows", across_moves
        )
        for i in range(2)
    )
    home_tags, own_tags, round_tags, across_tags = tags_for(
        clusters,
        jnp.stack([which, me % 2, receives.astype(jnp.int32)]),
        band,
        list_id[None],
        slot[None],
        [value[None] for value in passed],
    )

    best = jnp.full((1, rows_dev), -1.0, jnp.float32)
    best, _ = meet([quarter], own_tags, homes, home_tags, best, which, same=True)
    best, round_best = meet([round_rows], round_tags, homes, home_tags, best, which)
    best, early = meet([third], across_tags, homes, home_tags, best, receives.astype(jnp.int32), ready=True, gated=True)
    round_best, best = lax.optimization_barrier((round_best, best))
    round_best = lax.ppermute(round_best, "rows", [(b, a) for a, b in round_moves])
    round_best, best = lax.optimization_barrier((round_best, best))
    best, across_best = meet(
        [fourth], across_tags, homes, home_tags, best, receives.astype(jnp.int32), ready=True, offset=half, before=early, gated=True
    )

    chip, core = lax.axis_index("pairs"), lax.axis_index("sub")
    swap_cores = [(i, cores - 1 - i) for i in range(cores)]
    shared = lax.ppermute(across_best, "sub", swap_cores)
    shared = jnp.concatenate(
        [jnp.where(core == 0, across_best, shared), jnp.where(core == 0, shared, across_best)], axis=1
    )
    here = lax.dynamic_slice_in_dim(best, which * band, band, 1)
    best = lax.dynamic_update_slice_in_dim(best, jnp.maximum(here, round_best), which * band, 1)
    back = lax.ppermute(
        jnp.broadcast_to(shared, (4, cores * band)),
        ("rows", "pairs", "sub"),
        [
            ((b * chips + x) * cores + c, (a * chips + (x ^ c)) * cores + c)
            for a, b in across_moves
            for x in range(chips)
            for c in range(cores)
        ],
    )[:1]
    back = jnp.where(receives, -1.0, back)
    swapped = lax.ppermute(best, "pairs", [(i, chips - 1 - i) for i in range(chips)])
    first = (chip ^ core) * cores * band
    here = lax.dynamic_slice_in_dim(best, first, cores * band, 1)
    best = lax.dynamic_update_slice_in_dim(best, jnp.maximum(here, back), first, 1)
    best = jnp.maximum(best, swapped)
    best = jnp.maximum(best, lax.ppermute(best, "sub", swap_cores))
    return best.reshape(rows_dev)


def on_device(embeddings, slot, list_id):
    if lax.axis_size("rows") == SPAN:
        return dense(embeddings, slot, list_id)
    return banded(embeddings, slot, list_id)


def solution(mesh):
    return jax.shard_map(
        on_device,
        mesh=mesh,
        in_specs=(P(("groups", "rows"), None), P(("groups", "rows")), P(("groups", "rows"))),
        out_specs=P(("groups", "rows")),
        check_vma=False,
    )
```

```python
import functools

import jax
import jax.numpy as jnp
from jax import lax
from jax.experimental import pallas as pl
from jax.experimental.pallas import tpu as pltpu
from jax.sharding import PartitionSpec as P

SPAN = 4
POSITIONS_PER_CLUSTER = 1024
LANES = 128
TILE = 256
VMEM_BYTES = 32 * 1024 * 1024


def shifted(value, axis, by):
    length = lax.axis_size(axis)
    pairs = [(i, i + by) for i in range(length) if 0 <= i + by < length]
    return lax.ppermute(value, axis, pairs)


def placed(received, codes, rows_dev):
    flat = received.reshape(-1, received.shape[-1])
    flat_codes = codes.reshape(-1)
    target = jnp.where(flat_codes >= 0, flat_codes, rows_dev)
    return jnp.zeros((rows_dev, flat.shape[1]), flat.dtype).at[target].set(flat, mode="drop")


def masked_scores(owned, tags, far_rows, far_tags):
    scores = lax.dot_general(
        owned, far_rows, (((1,), (1,)), ((), ())), preferred_element_type=jnp.float32
    )
    return jnp.where(tags[:, None] == far_tags[None, :], scores, -1.0)


def banded(embeddings, slot, list_id):
    rows_dev = embeddings.shape[0]
    width = embeddings.shape[1]
    peers = lax.axis_size("rows")
    capacity = 3 * (rows_dev // peers) // 2
    wide = embeddings.astype(jnp.float32)
    unit = (wide / jnp.sqrt(jnp.sum(wide * wide, axis=1, keepdims=True) + 1e-06)).astype(
        jnp.bfloat16
    )
    owner = slot // rows_dev
    local = slot - owner * rows_dev
    onehot = (owner[:, None] == jnp.arange(peers, dtype=jnp.int32)[None, :]).astype(jnp.int32)
    order = jnp.sum((jnp.cumsum(onehot, axis=0) - onehot) * onehot, axis=1)
    send_code = jnp.full((peers, capacity), -1, jnp.int32).at[owner, order].set(local)
    pieces = lax.axis_size(("pairs", "sub"))
    which = lax.axis_index(("pairs", "sub"))
    send_rows = jnp.zeros((peers, capacity, width), jnp.bfloat16).at[owner, order].set(unit)
    got_rows, got_code = (
        lax.all_to_all(send_rows, "rows", split_axis=0, concat_axis=0, tiled=True),
        lax.all_to_all(send_code, "rows", split_axis=0, concat_axis=0, tiled=True),
    )
    owned = placed(got_rows, got_code, rows_dev)
    tags = list_id + 1
    band = rows_dev // pieces
    columns = lax.dynamic_slice_in_dim(owned, which * band, band, 0)
    column_tags = lax.dynamic_slice_in_dim(tags, which * band, band, 0)
    row_index = jnp.arange(rows_dev, dtype=jnp.int32)
    column_index = which * band + jnp.arange(band, dtype=jnp.int32)
    near = masked_scores(owned, tags, columns, column_tags)
    near = jnp.where(row_index[:, None] == column_index[None, :], -1.0, near)
    best = jnp.max(near, axis=1)
    offsets = list(range(1 - SPAN, 0)) + list(range(1, SPAN))
    for step in offsets:
        far_rows, far_tags = shifted((columns, column_tags), "rows", step)
        best = jnp.maximum(best, jnp.max(masked_scores(owned, tags, far_rows, far_tags), axis=1))
    answer = lax.pmax(best, ("pairs", "sub"))
    values = jnp.where(got_code >= 0, answer[jnp.clip(got_code, 0, rows_dev - 1)], 0.0)
    homeward = lax.all_to_all(values, "rows", split_axis=0, concat_axis=0, tiled=True)
    return homeward[owner, order]


def normalised(rows):
    wide = rows.astype(jnp.float32)
    squares = jnp.sum(wide * wide, axis=1, keepdims=True)
    return (wide * (1.0 / jnp.sqrt(squares + 1e-06))).astype(jnp.bfloat16)


def unit_kernel(rows_ref, unit_ref):
    unit_ref[...] = normalised(rows_ref[...])


def unit_rows(rows):
    count, width = rows.shape
    step = min(count, 1024)
    return pl.pallas_call(
        unit_kernel,
        grid=(count // step,),
        in_specs=[pl.BlockSpec((step, width), lambda i: (i, 0))],
        out_specs=pl.BlockSpec((step, width), lambda i: (i, 0)),
        out_shape=jax.ShapeDtypeStruct(rows.shape, jnp.bfloat16),
        cost_estimate=pl.CostEstimate(
            flops=4 * count * width, bytes_accessed=4 * count * width, transcendentals=count
        ),
    )(rows)


def tags_kernel(clusters, place_ref, list_ref, slot_ref, *refs):
    passed_refs, (home_ref, own_ref, left_ref, across_ref) = refs[:-4], refs[-4:]
    which, odd, receives = place_ref[0], place_ref[1] == 1, place_ref[2] == 1
    total = list_ref.shape[1]
    band = own_ref.shape[0]

    def arrived(piece, lanes):
        value = passed_refs[0][:, lanes]
        for flip in range(1, len(passed_refs)):
            value = jnp.where(which == piece ^ flip, passed_refs[flip][:, lanes], value)
        return value

    lists = [list_ref[...]] + [arrived(piece, pl.ds(0, total)) for piece in range(len(passed_refs) - 1)]
    lists = jnp.concatenate([ids[:, i : i + LANES] for ids in lists for i in range(0, total, LANES)])
    starts = [jnp.sum((lists < k).astype(jnp.int32)) for k in range(1, clusters)]

    def tags_of(positions):
        return sum((positions >= start).astype(jnp.int32) for start in starts)

    def column(tags):
        return jnp.broadcast_to(tags, (LANES, band)).T

    mine = pl.multiple_of(which * band, band)
    slots = pl.ds(total + mine, band)
    home_ref[...] = tags_of(slot_ref[...])
    own_ref[...] = column(tags_of(slot_ref[:, pl.ds(mine, band)]))
    left_ref[...] = column(tags_of(jnp.where(odd, arrived(0, slots), arrived(2, slots))))
    across_ref[...] = column(jnp.where(receives, tags_of(arrived(1, slots)), -1))


def tags_for(clusters, place, band, list_id, slot, passed):
    vmem = pl.BlockSpec(memory_space=pltpu.VMEM)
    columns = jax.ShapeDtypeStruct((band, LANES), jnp.int32)
    total = slot.shape[1]
    return pl.pallas_call(
        functools.partial(tags_kernel, clusters),
        in_specs=[pl.BlockSpec(memory_space=pltpu.SMEM)] + [vmem] * (2 + len(passed)),
        out_specs=[vmem] * 4,
        out_shape=[jax.ShapeDtypeStruct((1, total), jnp.int32)] + [columns] * 3,
        cost_estimate=pl.CostEstimate(flops=total * 32, bytes_accessed=total * 32, transcendentals=0),
    )(place, list_id, slot, *passed)


def meet_rows(same, ready, offset, extra, which_ref, best_ref, home_ref, home_tags_ref, tags_ref, *refs):
    other_refs, (home_best_ref, other_best_ref) = refs[: -2 - extra], refs[-2:]
    homes = home_ref.shape[0]
    unit = jnp.concatenate([ref[...] if ready else normalised(ref[...]) for ref in other_refs])
    others = unit.shape[0]
    tags = tags_ref[pl.ds(offset, others), :1]
    folded = jnp.full((others, LANES), -1.0, jnp.float32)
    if same:
        place = which_ref[0] * others + lax.broadcasted_iota(jnp.int32, (others, TILE), 0)
    for start in range(0, homes, TILE):
        here = pl.ds(start, TILE)
        scores = lax.dot_general(
            unit, home_ref[here, :], (((1,), (1,)), ((), ())), preferred_element_type=jnp.float32
        )
        keep = tags == home_tags_ref[:, here]
        if same:
            keep &= place != start + lax.broadcasted_iota(jnp.int32, (others, TILE), 1)
        scores = jnp.where(keep, scores, -1.0)
        home_best_ref[:, here] = jnp.maximum(best_ref[:, here], jnp.max(scores, axis=0, keepdims=True))
        for lane in range(0, TILE, LANES):
            folded = jnp.maximum(folded, scores[:, lane : lane + LANES])
    if extra:
        other_best_ref[:, :offset] = refs[len(other_refs)][...]
    other_best_ref[:, offset if extra else 0 :] = jnp.max(folded.T, axis=0, keepdims=True)


def meet_kernel(gated, same, ready, offset, extra, flag_ref, best_ref, *refs):
    if not gated:
        meet_rows(same, ready, offset, extra, flag_ref, best_ref, *refs)
        return

    @pl.when(flag_ref[0] == 1)
    def _():
        meet_rows(same, ready, offset, extra, flag_ref, best_ref, *refs)

    @pl.when(flag_ref[0] != 1)
    def _():
        refs[-2][...] = best_ref[...]
        refs[-1][...] = jnp.full(refs[-1].shape, -1.0, jnp.float32)


def meet(others, tags, homes, home_tags, best, flag, same=False, ready=False, offset=0, before=None, gated=False):
    count = sum(rows.shape[0] for rows in others)
    total, width = homes.shape
    before = [] if before is None else [before]
    vmem = pl.BlockSpec(memory_space=pltpu.VMEM)
    return pl.pallas_call(
        functools.partial(meet_kernel, gated, same, ready, offset, len(before)),
        in_specs=[pl.BlockSpec(memory_space=pltpu.SMEM)] + [vmem] * (4 + len(others) + len(before)),
        out_specs=[vmem, vmem],
        out_shape=[
            jax.ShapeDtypeStruct((1, total), jnp.float32),
            jax.ShapeDtypeStruct((1, count + (offset if before else 0)), jnp.float32),
        ],
        compiler_params=pltpu.CompilerParams(vmem_limit_bytes=VMEM_BYTES),
        cost_estimate=pl.CostEstimate(
            flops=2 * count * total * width,
            bytes_accessed=2 * (count + total) * width,
            transcendentals=count,
        ),
    )(flag.reshape(1), best, homes, home_tags, tags, *others, *before)


def dense(embeddings, slot, list_id):
    rows_dev = embeddings.shape[0]
    peers = lax.axis_size("rows")
    me = lax.axis_index("rows")
    pieces = lax.axis_size(("pairs", "sub"))
    which = lax.axis_index(("pairs", "sub"))
    band = rows_dev // pieces
    half = band // 2
    clusters = peers * rows_dev // POSITIONS_PER_CLUSTER
    round_moves = [(i, (i + 1) % peers) for i in range(peers)]
    across_moves = [(0, 2), (3, 1)]
    receives = (me == 1) | (me == 2)

    cores = lax.axis_size("sub")
    chips = pieces // cores

    def pieces_of(rows, length):
        return rows.reshape(-1, length, rows.shape[1])

    passed = lax.ppermute(
        jnp.concatenate([list_id, slot]),
        ("rows", "pairs", "sub"),
        [(i * pieces + p, (i ^ ((1, 2, 3, 3)[p])) * pieces + p) for i in range(peers) for p in range(peers)],
    )
    quarter = lax.dynamic_index_in_dim(pieces_of(embeddings, band), which, 0, keepdims=False)
    quarter, embeddings, passed = lax.optimization_barrier((quarter, embeddings, passed))
    round_rows = lax.ppermute(quarter, "rows", round_moves)
    passed = [passed] + [
        lax.ppermute(passed, ("pairs", "sub"), [(p, p ^ flip) for p in range(pieces)])
        for flip in range(1, pieces)
    ]

    homes = unit_rows(embeddings)
    third, fourth = (lax.ppermute(rows, "rows", across_moves) for rows in (quarter[:half], quarter[half:]))
    home_tags, own_tags, round_tags, across_tags = tags_for(
        clusters,
        jnp.stack([which, me % 2, receives.astype(jnp.int32)]),
        band,
        list_id[None],
        slot[None],
        [value[None] for value in passed],
    )

    best = jnp.full((1, rows_dev), -1.0, jnp.float32)
    best, _ = meet([quarter], own_tags, homes, home_tags, best, which, same=True)
    best, round_best = meet([round_rows], round_tags, homes, home_tags, best, which)
    best, early = meet([third], across_tags, homes, home_tags, best, receives.astype(jnp.int32), gated=True)
    round_best, best = lax.optimization_barrier((round_best, best))
    round_best = lax.ppermute(round_best, "rows", [(b, a) for a, b in round_moves])
    round_best, best = lax.optimization_barrier((round_best, best))
    best, across_best = meet(
        [fourth], across_tags, homes, home_tags, best, receives.astype(jnp.int32), offset=half, before=early, gated=True
    )

    chip, core = lax.axis_index("pairs"), lax.axis_index("sub")
    swap_cores = [(i, cores - 1 - i) for i in range(cores)]
    shared = lax.ppermute(across_best, "sub", swap_cores)
    shared = jnp.concatenate(
        [jnp.where(core == 0, across_best, shared), jnp.where(core == 0, shared, across_best)], axis=1
    )
    here = lax.dynamic_slice_in_dim(best, which * band, band, 1)
    best = lax.dynamic_update_slice_in_dim(best, jnp.maximum(here, round_best), which * band, 1)
    back = lax.ppermute(
        jnp.broadcast_to(shared, (4, cores * band)),
        ("rows", "pairs", "sub"),
        [
            ((b * chips + x) * cores + c, (a * chips + (x ^ c)) * cores + c)
            for a, b in across_moves
            for x in range(chips)
            for c in range(cores)
        ],
    )[:1]
    back = jnp.where(receives, -1.0, back)
    swapped = lax.ppermute(best, "pairs", [(i, chips - 1 - i) for i in range(chips)])
    first = (chip ^ core) * cores * band
    here = lax.dynamic_slice_in_dim(best, first, cores * band, 1)
    best = lax.dynamic_update_slice_in_dim(best, jnp.maximum(here, back), first, 1)
    best = jnp.maximum(best, swapped)
    best = jnp.maximum(best, lax.ppermute(best, "sub", swap_cores))
    return best.reshape(rows_dev)


def on_device(embeddings, slot, list_id):
    if lax.axis_size("rows") == SPAN:
        return dense(embeddings, slot, list_id)
    return banded(embeddings, slot, list_id)


def solution(mesh):
    return jax.shard_map(
        on_device,
        mesh=mesh,
        in_specs=(P(("groups", "rows"), None), P(("groups", "rows")), P(("groups", "rows"))),
        out_specs=P(("groups", "rows")),
        check_vma=False,
    )
```

```python
import functools

import jax
import jax.numpy as jnp
from jax import lax
from jax.experimental import pallas as pl
from jax.experimental.pallas import tpu as pltpu
from jax.sharding import PartitionSpec as P

SPAN = 4
POSITIONS_PER_CLUSTER = 1024
LANES = 128
TILE = 256
VMEM_BYTES = 32 * 1024 * 1024


def shifted(value, axis, by):
    length = lax.axis_size(axis)
    pairs = [(i, i + by) for i in range(length) if 0 <= i + by < length]
    return lax.ppermute(value, axis, pairs)


def placed(received, codes, rows_dev):
    flat = received.reshape(-1, received.shape[-1])
    flat_codes = codes.reshape(-1)
    target = jnp.where(flat_codes >= 0, flat_codes, rows_dev)
    return jnp.zeros((rows_dev, flat.shape[1]), flat.dtype).at[target].set(flat, mode="drop")


def masked_scores(owned, tags, far_rows, far_tags):
    scores = lax.dot_general(
        owned, far_rows, (((1,), (1,)), ((), ())), preferred_element_type=jnp.float32
    )
    return jnp.where(tags[:, None] == far_tags[None, :], scores, -1.0)


def banded(embeddings, slot, list_id):
    rows_dev = embeddings.shape[0]
    width = embeddings.shape[1]
    peers = lax.axis_size("rows")
    capacity = 3 * (rows_dev // peers) // 2
    wide = embeddings.astype(jnp.float32)
    unit = (wide / jnp.sqrt(jnp.sum(wide * wide, axis=1, keepdims=True) + 1e-06)).astype(
        jnp.bfloat16
    )
    owner = slot // rows_dev
    local = slot - owner * rows_dev
    onehot = (owner[:, None] == jnp.arange(peers, dtype=jnp.int32)[None, :]).astype(jnp.int32)
    order = jnp.sum((jnp.cumsum(onehot, axis=0) - onehot) * onehot, axis=1)
    send_code = jnp.full((peers, capacity), -1, jnp.int32).at[owner, order].set(local)
    pieces = lax.axis_size(("pairs", "sub"))
    which = lax.axis_index(("pairs", "sub"))
    send_rows = jnp.zeros((peers, capacity, width), jnp.bfloat16).at[owner, order].set(unit)
    got_rows, got_code = (
        lax.all_to_all(send_rows, "rows", split_axis=0, concat_axis=0, tiled=True),
        lax.all_to_all(send_code, "rows", split_axis=0, concat_axis=0, tiled=True),
    )
    owned = placed(got_rows, got_code, rows_dev)
    tags = list_id + 1
    band = rows_dev // pieces
    columns = lax.dynamic_slice_in_dim(owned, which * band, band, 0)
    column_tags = lax.dynamic_slice_in_dim(tags, which * band, band, 0)
    row_index = jnp.arange(rows_dev, dtype=jnp.int32)
    column_index = which * band + jnp.arange(band, dtype=jnp.int32)
    near = masked_scores(owned, tags, columns, column_tags)
    near = jnp.where(row_index[:, None] == column_index[None, :], -1.0, near)
    best = jnp.max(near, axis=1)
    offsets = list(range(1 - SPAN, 0)) + list(range(1, SPAN))
    for step in offsets:
        far_rows, far_tags = shifted((columns, column_tags), "rows", step)
        best = jnp.maximum(best, jnp.max(masked_scores(owned, tags, far_rows, far_tags), axis=1))
    answer = lax.pmax(best, ("pairs", "sub"))
    values = jnp.where(got_code >= 0, answer[jnp.clip(got_code, 0, rows_dev - 1)], 0.0)
    homeward = lax.all_to_all(values, "rows", split_axis=0, concat_axis=0, tiled=True)
    return homeward[owner, order]


def normalised(rows):
    wide = rows.astype(jnp.float32)
    squares = jnp.sum(wide * wide, axis=1, keepdims=True)
    return (wide * (1.0 / jnp.sqrt(squares + 1e-06))).astype(jnp.bfloat16)


def unit_kernel(rows_ref, unit_ref):
    unit_ref[...] = normalised(rows_ref[...])


def unit_rows(rows):
    count, width = rows.shape
    step = min(count, 1024)
    return pl.pallas_call(
        unit_kernel,
        grid=(count // step,),
        in_specs=[pl.BlockSpec((step, width), lambda i: (i, 0))],
        out_specs=pl.BlockSpec((step, width), lambda i: (i, 0)),
        out_shape=jax.ShapeDtypeStruct(rows.shape, jnp.bfloat16),
        cost_estimate=pl.CostEstimate(
            flops=4 * count * width, bytes_accessed=4 * count * width, transcendentals=count
        ),
    )(rows)


def tags_kernel(clusters, place_ref, list_ref, slot_ref, *refs):
    passed_refs, (home_ref, own_ref, left_ref, across_ref) = refs[:-4], refs[-4:]
    which, odd, receives = place_ref[0], place_ref[1] == 1, place_ref[2] == 1
    total = list_ref.shape[1]
    band = own_ref.shape[0]

    def arrived(piece, lanes):
        value = passed_refs[0][:, lanes]
        for flip in range(1, len(passed_refs)):
            value = jnp.where(which == piece ^ flip, passed_refs[flip][:, lanes], value)
        return value

    lists = [list_ref[...]] + [arrived(piece, pl.ds(0, total)) for piece in range(len(passed_refs) - 1)]
    lists = jnp.concatenate([ids[:, i : i + LANES] for ids in lists for i in range(0, total, LANES)])
    starts = [jnp.sum((lists < k).astype(jnp.int32)) for k in range(1, clusters)]

    def tags_of(positions):
        return sum((positions >= start).astype(jnp.int32) for start in starts)

    def column(tags):
        return jnp.broadcast_to(tags, (LANES, band)).T

    mine = pl.multiple_of(which * band, band)
    slots = pl.ds(total + mine, band)
    home_ref[...] = tags_of(slot_ref[...])
    own_ref[...] = column(tags_of(slot_ref[:, pl.ds(mine, band)]))
    left_ref[...] = column(tags_of(jnp.where(odd, arrived(0, slots), arrived(2, slots))))
    across_ref[...] = column(jnp.where(receives, tags_of(arrived(1, slots)), -1))


def tags_for(clusters, place, band, list_id, slot, passed):
    vmem = pl.BlockSpec(memory_space=pltpu.VMEM)
    columns = jax.ShapeDtypeStruct((band, LANES), jnp.int32)
    total = slot.shape[1]
    return pl.pallas_call(
        functools.partial(tags_kernel, clusters),
        in_specs=[pl.BlockSpec(memory_space=pltpu.SMEM)] + [vmem] * (2 + len(passed)),
        out_specs=[vmem] * 4,
        out_shape=[jax.ShapeDtypeStruct((1, total), jnp.int32)] + [columns] * 3,
        cost_estimate=pl.CostEstimate(flops=total * 32, bytes_accessed=total * 32, transcendentals=0),
    )(place, list_id, slot, *passed)


def meet_rows(same, ready, offset, extra, which_ref, best_ref, home_ref, home_tags_ref, tags_ref, *refs):
    other_refs, (home_best_ref, other_best_ref) = refs[: -2 - extra], refs[-2:]
    homes = home_ref.shape[0]
    unit = jnp.concatenate([ref[...] if ready else normalised(ref[...]) for ref in other_refs])
    others = unit.shape[0]
    tags = tags_ref[pl.ds(offset, others), :1]
    folded = jnp.full((others, LANES), -1.0, jnp.float32)
    if same:
        place = which_ref[0] * others + lax.broadcasted_iota(jnp.int32, (others, TILE), 0)
    for start in range(0, homes, TILE):
        here = pl.ds(start, TILE)
        scores = lax.dot_general(
            unit, home_ref[here, :], (((1,), (1,)), ((), ())), preferred_element_type=jnp.float32
        )
        keep = tags == home_tags_ref[:, here]
        if same:
            keep &= place != start + lax.broadcasted_iota(jnp.int32, (others, TILE), 1)
        scores = jnp.where(keep, scores, -1.0)
        home_best_ref[:, here] = jnp.maximum(best_ref[:, here], jnp.max(scores, axis=0, keepdims=True))
        for lane in range(0, TILE, LANES):
            folded = jnp.maximum(folded, scores[:, lane : lane + LANES])
    if extra:
        other_best_ref[:, :offset] = refs[len(other_refs)][...]
    other_best_ref[:, offset if extra else 0 :] = jnp.max(folded.T, axis=0, keepdims=True)


def meet_kernel(gated, same, ready, offset, extra, flag_ref, best_ref, *refs):
    if not gated:
        meet_rows(same, ready, offset, extra, flag_ref, best_ref, *refs)
        return

    @pl.when(flag_ref[0] == 1)
    def _():
        meet_rows(same, ready, offset, extra, flag_ref, best_ref, *refs)

    @pl.when(flag_ref[0] != 1)
    def _():
        refs[-2][...] = best_ref[...]
        refs[-1][...] = jnp.full(refs[-1].shape, -1.0, jnp.float32)


def meet(others, tags, homes, home_tags, best, flag, same=False, ready=False, offset=0, before=None, gated=False):
    count = sum(rows.shape[0] for rows in others)
    total, width = homes.shape
    before = [] if before is None else [before]
    vmem = pl.BlockSpec(memory_space=pltpu.VMEM)
    return pl.pallas_call(
        functools.partial(meet_kernel, gated, same, ready, offset, len(before)),
        in_specs=[pl.BlockSpec(memory_space=pltpu.SMEM)] + [vmem] * (4 + len(others) + len(before)),
        out_specs=[vmem, vmem],
        out_shape=[
            jax.ShapeDtypeStruct((1, total), jnp.float32),
            jax.ShapeDtypeStruct((1, count + (offset if before else 0)), jnp.float32),
        ],
        compiler_params=pltpu.CompilerParams(vmem_limit_bytes=VMEM_BYTES),
        cost_estimate=pl.CostEstimate(
            flops=2 * count * total * width,
            bytes_accessed=2 * (count + total) * width,
            transcendentals=count,
        ),
    )(flag.reshape(1), best, homes, home_tags, tags, *others, *before)


def dense(embeddings, slot, list_id):
    rows_dev = embeddings.shape[0]
    peers = lax.axis_size("rows")
    me = lax.axis_index("rows")
    pieces = lax.axis_size(("pairs", "sub"))
    which = lax.axis_index(("pairs", "sub"))
    band = rows_dev // pieces
    half = band // 2
    clusters = peers * rows_dev // POSITIONS_PER_CLUSTER
    round_moves = [(i, (i + 1) % peers) for i in range(peers)]
    across_moves = [(0, 2), (3, 1)]
    receives = (me == 1) | (me == 2)

    cores = lax.axis_size("sub")
    chips = pieces // cores

    def pieces_of(rows, length):
        return rows.reshape(-1, length, rows.shape[1])

    passed = lax.ppermute(
        jnp.concatenate([list_id, slot]),
        ("rows", "pairs", "sub"),
        [(i * pieces + p, (i ^ ((1, 2, 3, 3)[p])) * pieces + p) for i in range(peers) for p in range(peers)],
    )
    quarter = lax.dynamic_index_in_dim(pieces_of(embeddings, band), which, 0, keepdims=False)
    quarter, embeddings, passed = lax.optimization_barrier((quarter, embeddings, passed))
    round_rows = lax.ppermute(quarter, "rows", round_moves)
    passed = [passed] + [
        lax.ppermute(passed, ("pairs", "sub"), [(p, p ^ flip) for p in range(pieces)])
        for flip in range(1, pieces)
    ]

    homes = unit_rows(embeddings)
    third = lax.ppermute(quarter[:half], "rows", across_moves)
    fourth = lax.dynamic_index_in_dim(pieces_of(homes, half), 2 * which + 1, 0, keepdims=False)
    fourth = lax.ppermute(fourth, "rows", across_moves)
    home_tags, own_tags, round_tags, across_tags = tags_for(
        clusters,
        jnp.stack([which, me % 2, receives.astype(jnp.int32)]),
        band,
        list_id[None],
        slot[None],
        [value[None] for value in passed],
    )

    best = jnp.full((1, rows_dev), -1.0, jnp.float32)
    best, _ = meet([quarter], own_tags, homes, home_tags, best, which, same=True)
    best, round_best = meet([round_rows], round_tags, homes, home_tags, best, which)
    best, early = meet([third], across_tags, homes, home_tags, best, receives.astype(jnp.int32), gated=True)
    round_best, best = lax.optimization_barrier((round_best, best))
    round_best = lax.ppermute(round_best, "rows", [(b, a) for a, b in round_moves])
    round_best, best = lax.optimization_barrier((round_best, best))
    best, across_best = meet(
        [fourth], across_tags, homes, home_tags, best, receives.astype(jnp.int32), ready=True, offset=half, before=early, gated=True
    )

    chip, core = lax.axis_index("pairs"), lax.axis_index("sub")
    swap_cores = [(i, cores - 1 - i) for i in range(cores)]
    shared = lax.ppermute(across_best, "sub", swap_cores)
    shared = jnp.concatenate(
        [jnp.where(core == 0, across_best, shared), jnp.where(core == 0, shared, across_best)], axis=1
    )
    here = lax.dynamic_slice_in_dim(best, which * band, band, 1)
    best = lax.dynamic_update_slice_in_dim(best, jnp.maximum(here, round_best), which * band, 1)
    back = lax.ppermute(
        jnp.broadcast_to(shared, (4, cores * band)),
        ("rows", "pairs", "sub"),
        [
            ((b * chips + x) * cores + c, (a * chips + (x ^ c)) * cores + c)
            for a, b in across_moves
            for x in range(chips)
            for c in range(cores)
        ],
    )[:1]
    back = jnp.where(receives, -1.0, back)
    swapped = lax.ppermute(best, "pairs", [(i, chips - 1 - i) for i in range(chips)])
    first = (chip ^ core) * cores * band
    here = lax.dynamic_slice_in_dim(best, first, cores * band, 1)
    best = lax.dynamic_update_slice_in_dim(best, jnp.maximum(here, back), first, 1)
    best = jnp.maximum(best, swapped)
    best = jnp.maximum(best, lax.ppermute(best, "sub", swap_cores))
    return best.reshape(rows_dev)


def on_device(embeddings, slot, list_id):
    if lax.axis_size("rows") == SPAN:
        return dense(embeddings, slot, list_id)
    return banded(embeddings, slot, list_id)


def solution(mesh):
    return jax.shard_map(
        on_device,
        mesh=mesh,
        in_specs=(P(("groups", "rows"), None), P(("groups", "rows")), P(("groups", "rows"))),
        out_specs=P(("groups", "rows")),
        check_vma=False,
    )
```
